512 devices in a mesh: blk: 32 (over x_lo, z), resp: 4 (over x_hi, core), batch: 4 (over y).
Axes of the slice: x: 4 (x_hi: 2, x_lo: 2; x = x_hi * 2 + x_lo), y: 4, z: 16, core: 2. Of those that a mesh axis runs over, the one named last changes fastest.
Arguments:
- prompt_query: bfloat16 [12288, 512], P(('batch', 'blk'), 'resp'), parts along dimension 0, may hold values from -22 to 22
- answer_query: bfloat16 [8, 2048, 512], P('batch', 'blk', 'resp'), parts along dimension 0, may hold values from -22 to 22
- prompt_kv: bfloat16 [12288, 256], P(('batch', 'blk')), parts along dimension 0, may hold values from -5 to 5
- answer_kv: bfloat16 [8, 2048, 256], P('batch', 'blk'), parts along dimension 0, may hold values from -5 to 5
- prompt_grad: bfloat16 [12288, 512], P(('batch', 'blk'), 'resp'), parts along dimension 0, may hold values from -6 to 6
- answer_grad: bfloat16 [8, 2048, 512], P('batch', 'blk', 'resp'), parts along dimension 0, may hold values from -6 to 6
- lengths: int32 [12], P('batch'), parts along dimension 0, may hold values from 512 to 3072, as said below
Outputs:
- prompt_out: bfloat16 [12288, 512], P(('batch', 'blk'), 'resp'), parts along dimension 0
- answer_out: bfloat16 [8, 2048, 512], P('batch', 'blk', 'resp'), parts along dimension 0
- prompt_query_grad: bfloat16 [12288, 512], P(('batch', 'blk'), 'resp'), parts along dimension 0
- answer_query_grad: bfloat16 [8, 2048, 512], P('batch', 'blk', 'resp'), parts along dimension 0
- prompt_kv_grad: bfloat16 [12288, 256], P(('batch', 'blk')), parts along dimension 0
- answer_kv_grad: bfloat16 [8, 2048, 256], P('batch', 'blk'), parts along dimension 0
The draws below stay inside these ranges and needn't reach their ends.
There are 4 independent parts, one for each index of `batch`. The reference program is written for one: setup_inputs(seed, part) draws one part's arguments, and reference() takes and returns one part's arrays. A program takes and returns all parts, laid end to end along the dimension named above; each array names one. Nothing has to cross between parts.
Inputs may be any that keep to these rules, and one draw needn't show every extreme that they name: lengths[0] is the prompt's length and equals 3072; lengths[1] and lengths[2] lie from 512 to 2048, and one of them is exactly 2048.
All inputs are finite; a program needn't handle non-finite values.
Results may differ from the reference program's by a relative error of at most 0.005.
Values may be sent and summed in bfloat16 or wider, within the bound.
A program may use at most 64 MiB of HBM per device.

```python
import math
import jax
import jax.numpy as jnp
from jax import lax

HEAD_DIM = 128
HEADS = 4
PROMPT = 3072
ANSWER = 2048


def draw_prompt_query(key, part):
    key = jax.random.fold_in(key, 1)
    base = jnp.clip(2.0 * jax.random.normal(key, (PROMPT, HEADS * HEAD_DIM), jnp.float32), -8.0, 8.0)
    return base.astype(jnp.bfloat16)


def draw_answer_query(key, part):
    key = jax.random.fold_in(key, 2)
    base = jnp.clip(2.0 * jax.random.normal(key, (2, ANSWER, HEADS * HEAD_DIM), jnp.float32), -8.0, 8.0)
    return base.astype(jnp.bfloat16)


def draw_prompt_kv(key, part):
    key = jax.random.fold_in(key, 3)
    base = jnp.clip(jax.random.normal(key, (PROMPT, 2 * HEAD_DIM), jnp.float32), -5.0, 5.0)
    return base.astype(jnp.bfloat16)


def draw_answer_kv(key, part):
    key = jax.random.fold_in(key, 4)
    base = jnp.clip(jax.random.normal(key, (2, ANSWER, 2 * HEAD_DIM), jnp.float32), -5.0, 5.0)
    return base.astype(jnp.bfloat16)


def draw_lengths(key, part):
    key = jax.random.fold_in(key, 9)
    prompt_length = jnp.array(PROMPT, jnp.int32)
    shorter = jax.random.randint(jax.random.fold_in(key, 2), (), ANSWER // 4, ANSWER + 1)
    flipped = jax.random.randint(jax.random.fold_in(key, 3), (), 0, 2)
    chosen = jnp.where(flipped == 0, ANSWER, shorter)
    rejected = jnp.where(flipped == 0, shorter, ANSWER)
    return jnp.stack([prompt_length, chosen, rejected]).astype(jnp.int32)


def steps_of(key, shape, split, least, largest):
    def one(dim, parts):
        heights = jax.random.uniform(jax.random.fold_in(jax.random.fold_in(key, 6), dim), (parts,), jnp.float32, least / len(split), largest / len(split))
        return jnp.repeat(jnp.exp(heights), shape[dim] // parts).reshape((-1,) + (1,) * (len(shape) - dim - 1))

    gain = one(*split[0])
    for cut in split[1:]:
        gain = gain * one(*cut)
    return gain


def centred(key, extent, deviation, reach, pieces=(), kind=jnp.bfloat16):
    result = deviation * jax.random.normal(key, extent, jnp.float32)
    if pieces:
        result = result * steps_of(key, extent, pieces, -0.22, 0.18)
    return jnp.clip(result, -reach, reach).astype(kind)


def setup_inputs(seed: int = 0, part: int = 0) -> dict:
    key_list = jax.random.split(jax.random.key(seed), 8)
    part_splits = jax.random.split(jax.random.fold_in(key_list[7], part), 8)
    return {
        "prompt_query": draw_prompt_query(jax.random.fold_in(jax.random.fold_in(key_list[7], part), 71), part),
        "answer_query": draw_answer_query(jax.random.fold_in(jax.random.fold_in(key_list[7], part), 71), part),
        "prompt_kv": draw_prompt_kv(jax.random.fold_in(jax.random.fold_in(key_list[7], part), 71), part),
        "answer_kv": draw_answer_kv(jax.random.fold_in(jax.random.fold_in(key_list[7], part), 71), part),
        "prompt_grad": centred(part_splits[4], (PROMPT, HEADS * HEAD_DIM), 1.0, 6.0, ((0, 32), (1, 4))),
        "answer_grad": centred(part_splits[5], (2, ANSWER, HEADS * HEAD_DIM), 1.0, 6.0, ((1, 32), (2, 4))),
        "lengths": draw_lengths(jax.random.fold_in(jax.random.fold_in(key_list[7], part), 71), part),
    }


def reference(prompt_query, answer_query, prompt_kv, answer_kv, prompt_grad, answer_grad, lengths):
    total = PROMPT + 2 * ANSWER
    kinds = jnp.concatenate([jnp.zeros((PROMPT,), jnp.int32), jnp.ones((ANSWER,), jnp.int32), jnp.full((ANSWER,), 2, jnp.int32)])
    places = jnp.concatenate([jnp.arange(PROMPT, dtype=jnp.int32), jnp.arange(ANSWER, dtype=jnp.int32), jnp.arange(ANSWER, dtype=jnp.int32)])
    bound = jnp.where(kinds == 0, lengths[0], jnp.where(kinds == 1, lengths[1], lengths[2]))
    valid = places < bound
    causal = places[None, :] <= places[:, None]
    prompt_key = kinds[None, :] == 0
    own_key = (kinds[None, :] == kinds[:, None]) & (kinds[:, None] != 0)
    allowed = valid[None, :] & (prompt_key & ((kinds[:, None] != 0) | causal) | own_key & causal)
    key_rows = jnp.concatenate([prompt_kv, answer_kv[0], answer_kv[1]], axis=0)
    keys_part = key_rows[:, :HEAD_DIM]
    values_part = key_rows[:, HEAD_DIM:]
    query_rows = jnp.concatenate([prompt_query, answer_query[0], answer_query[1]], axis=0)
    grad_rows = jnp.concatenate([prompt_grad, answer_grad[0], answer_grad[1]], axis=0)
    valid_float = valid.astype(jnp.float32)
    masked_rows = (grad_rows * valid_float[:, None]).astype(jnp.bfloat16)
    scaling = 1.0 / math.sqrt(HEAD_DIM)

    def one_head(head_index):
        start = (head_index * HEAD_DIM).astype(jnp.int32)
        queries = lax.dynamic_slice_in_dim(query_rows, start, HEAD_DIM, 1)
        masked = lax.dynamic_slice_in_dim(masked_rows, start, HEAD_DIM, 1)
        scores = jnp.dot(queries, keys_part.T, preferred_element_type=jnp.float32) * scaling
        hidden_scores = jnp.where(allowed, scores, -1e+30)
        row_max = lax.optimization_barrier(jnp.max(hidden_scores, axis=1))
        row_sum = lax.optimization_barrier(jnp.sum(jnp.where(allowed, jnp.exp(hidden_scores - row_max[:, None]), 0.0), axis=1))
        row_lse = row_max + jnp.log(row_sum)
        weights = jnp.exp(hidden_scores - row_lse[:, None])
        weights_b = weights.astype(jnp.bfloat16)
        attention = jnp.dot(weights_b, values_part, preferred_element_type=jnp.float32)
        output = (attention * valid_float[:, None]).astype(jnp.bfloat16)
        weight_grad = jnp.dot(masked, values_part.T, preferred_element_type=jnp.float32)
        deltas = lax.optimization_barrier(jnp.sum(weights * weight_grad, axis=1))
        score_grad = (weights * (weight_grad - deltas[:, None])).astype(jnp.bfloat16)
        query_grad = (jnp.dot(score_grad, keys_part, preferred_element_type=jnp.float32) * scaling).astype(jnp.bfloat16)
        key_grad = jnp.dot(score_grad.T, queries, preferred_element_type=jnp.float32)
        value_grad = jnp.dot(weights_b.T, masked, preferred_element_type=jnp.float32)
        return (output, query_grad, key_grad, value_grad)
    outputs, query_grads, key_grads, value_grads = lax.map(one_head, jnp.arange(HEADS, dtype=jnp.int32))
    output_rows = jnp.transpose(outputs, (1, 0, 2)).reshape(total, HEADS * HEAD_DIM)
    query_grad_rows = jnp.transpose(query_grads, (1, 0, 2)).reshape(total, HEADS * HEAD_DIM)
    key_grad = lax.optimization_barrier(jnp.sum(key_grads, axis=0)) * scaling
    value_grad = lax.optimization_barrier(jnp.sum(value_grads, axis=0))
    kv_grad = jnp.concatenate([key_grad, value_grad], axis=1).astype(jnp.bfloat16)
    prompt_out = output_rows[:PROMPT]
    answer_out = jnp.stack([output_rows[PROMPT:PROMPT + ANSWER], output_rows[PROMPT + ANSWER:]])
    prompt_query_grad = query_grad_rows[:PROMPT]
    answer_query_grad = jnp.stack([query_grad_rows[PROMPT:PROMPT + ANSWER], query_grad_rows[PROMPT + ANSWER:]])
    prompt_kv_grad = kv_grad[:PROMPT]
    answer_kv_grad = jnp.stack([kv_grad[PROMPT:PROMPT + ANSWER], kv_grad[PROMPT + ANSWER:]])
    return (prompt_out, answer_out, prompt_query_grad, answer_query_grad, prompt_kv_grad, answer_kv_grad)
```

```python
import math

import jax
import jax.numpy as jnp
from jax import lax
from jax.experimental import pallas as pl
from jax.experimental.pallas import tpu as pltpu
from jax.sharding import PartitionSpec as P

MESH = pl.DeviceIdType.MESH
F32 = jnp.float32
BF16 = jnp.bfloat16
HIDDEN = -1e30
FLOOR = -1e20
RING = 16
PR, AR = 48, 32
BLOCK = PR + 2 * AR
QP, QA = 96, 64
OWN = QP + 2 * QA
ROWS = 4 * OWN
NP, NA = 4 * QP, 4 * QA
GROUPS, WIDTH = 4, 4

GATHER = {1: 0, 3: 0, 2: 3, 4: 3, 6: 3, 5: 6, 7: 6, 8: 6}
REDUCE = {1: 0, 3: 0, 6: 0, 2: 3, 4: 3, 5: 6, 7: 6, 8: 6}
ORDER = [1, 3, 2, 4, 6, 5, 7]
READY = [[1, 3], [2, 4], [6, 5], [7, 8]]
DONE = [[7, 8], [5, 6], [2, 4], [3, 1]]


def children(tree, parent):
    return sorted([o for o, p in tree.items() if p == parent], reverse=True)


SIGNED = [0] * 16
for _i, _o in enumerate(ORDER):
    SIGNED[1 + 2 * _i], SIGNED[2 + 2 * _i] = -_o, _o
SIGNED[15] = 8


def slot_of(offset, core):
    if offset == 8:
        return 15
    return 1 + 2 * ORDER.index(offset) + core


def dot_last(a, b):
    return lax.dot_general(a, b, (((1,), (1,)), ((), ())), preferred_element_type=F32)


def dot_first(a, b):
    return lax.dot_general(a, b, (((0,), (0,)), ((), ())), preferred_element_type=F32)


def dot(a, b):
    return jnp.dot(a, b, preferred_element_type=F32)


def kernel(
    pq, aq, pkv, akv, pg, ag, lens,
    po, ao, pqg, aqg, pkvg, akvg,
    kv, qg, q_all, g_all, pp, dpp, pa, dpa, stat, ot, st, dqt, own_f, osend, orecv,
    part, sib_out, sib_in, rs_out, rs_in, fin,
    loc, kv_r, kv_s, kv_x, qg_r, qg_s, st_r, st_s, o_r, o_s, sib_r, sib_s, rs_r, rs_s, fin_r, fin_s,
):
    blk, resp = lax.axis_index("blk"), lax.axis_index("resp")
    lo, z = blk // RING, lax.rem(blk, RING)
    hi, c = resp // 2, lax.rem(resp, 2)
    x = hi * 2 + lo
    s = 1 - 2 * c
    scaling = 1.0 / math.sqrt(128)

    def ring(step):
        return {"blk": lo * RING + lax.rem(z + step + 2 * RING, RING), "resp": resp}

    def across(step, core):
        to = lax.rem(x + step + 4, 4)
        return {"blk": lax.rem(to, 2) * RING + z, "resp": (to // 2) * 2 + core}

    sibling = {"blk": blk, "resp": hi * 2 + 1 - c}

    def remote(src, dst, send, recv, to):
        return pltpu.make_async_remote_copy(
            src_ref=src, dst_ref=dst, send_sem=send, recv_sem=recv, device_id=to, device_id_type=MESH
        )

    def guard(offset, act):
        if offset == 8:
            pl.when(c == 0)(act)
        else:
            act()

    first_p = pl.multiple_of(hi * PR, PR)
    first_a = pl.multiple_of(hi * AR, AR)
    pairs = [
        (pkv.at[pl.ds(first_p, PR)], kv.at[0, pl.ds(0, PR)]),
        (akv.at[0, pl.ds(first_a, AR)], kv.at[0, pl.ds(PR, AR)]),
        (akv.at[1, pl.ds(first_a, AR)], kv.at[0, pl.ds(PR + AR, AR)]),
    ]
    for j, (p_ref, a_ref) in enumerate(((pq, aq), (pg, ag))):
        cols = pl.ds(128 * j, 128)
        pairs.append((p_ref, qg.at[x, pl.ds(0, QP), cols]))
        pairs.append((a_ref.at[0], qg.at[x, pl.ds(QP, QA), cols]))
        pairs.append((a_ref.at[1], qg.at[x, pl.ds(QP + QA, QA), cols]))
    loads = [pltpu.make_async_copy(a, b, loc.at[i]) for i, (a, b) in enumerate(pairs)]
    for load in loads:
        load.start()

    barrier = pltpu.get_barrier_semaphore()
    steps = sorted({o - p for o, p in GATHER.items()})
    senders = [ring(-s * d) for d in steps] + [across(d, c) for d in (1, 2, 3)] + [sibling]
    for device in senders:
        pl.semaphore_signal(barrier, inc=1, device_id=device, device_id_type=MESH)
    for load in loads:
        load.wait()
    pl.semaphore_wait(barrier, len(senders))

    def hop(o):
        p = GATHER[o]
        src = kv.at[0] if p == 0 else kv.at[slot_of(p, c)]
        mine = slot_of(o, c)
        return remote(src, kv.at[mine], kv_s.at[o], kv_r.at[mine], ring(s * (o - p)))

    def share(o):
        mine = slot_of(o, c)
        return remote(kv.at[mine], kv.at[mine], kv_x.at[o], kv_r.at[mine], sibling)

    def theirs(o):
        other = slot_of(o, 1 - c)
        pltpu.make_async_copy(kv.at[other], kv.at[other], kv_r.at[other]).wait()

    def arrive(o):
        def act():
            hop(o).wait_recv()
            for o2 in children(GATHER, o):
                guard(o2, lambda o2=o2: hop(o2).start())
            share(o).start()

        guard(o, act)

    def arrived(o):
        if o == 8:
            pl.when(c == 1)(lambda: theirs(8))
        else:
            theirs(o)

    for o in children(GATHER, 0):
        guard(o, lambda o=o: hop(o).start())
    sends_q = [
        remote(qg.at[x], qg.at[x], qg_s.at[d], qg_r.at[d], across(d, c)) for d in (1, 2, 3)
    ]
    for d in (1, 0, 2):
        sends_q[d].start()

    for o in READY[0]:
        arrive(o)
    for copy in sends_q:
        copy.wait_recv()

    for d in range(4):
        place = ((d % 2) * RING + z) * QA + lax.broadcasted_iota(jnp.int32, (QA, 128), 0)
        q_all[pl.ds(d * QP, QP)] = qg[d, pl.ds(0, QP), pl.ds(0, 128)]
        g_all[pl.ds(d * QP, QP)] = qg[d, pl.ds(0, QP), pl.ds(128, 128)]
        for k in range(2):
            rows = pl.ds(NP + k * NA + d * QA, QA)
            q_all[rows] = qg[d, pl.ds(QP + k * QA, QA), pl.ds(0, 128)]
            masked = jnp.where(
                place < lens[k + 1], qg[d, pl.ds(QP + k * QA, QA), pl.ds(128, 128)].astype(F32), 0.0
            )
            g_all[rows] = masked.astype(BF16)

    lane = lax.broadcasted_iota(jnp.int32, (1, NP), 1)
    which = (lane >= QP).astype(jnp.int32) + (lane >= 2 * QP) + (lane >= 3 * QP)
    q_place_p = (which & 1) * (RING * QP) + z * QP + lane - which * QP
    lane = lax.broadcasted_iota(jnp.int32, (1, NA), 1)
    which = (lane >= QA).astype(jnp.int32) + (lane >= 2 * QA) + (lane >= 3 * QA)
    q_place_a = (which & 1) * (RING * QA) + z * QA + lane - which * QA

    def key_ring(slot):
        off = jnp.int32(0)
        for k in range(1, 16):
            off = jnp.where(slot == k, SIGNED[k], off)
        return lo * RING + lax.rem(z + off + RING, RING)

    def kind_rows(ref, base, k):
        start, count = (0, PR) if k == 0 else (PR + (k - 1) * AR, AR)
        block = ref[pl.ds(base, WIDTH), pl.ds(start, count), :]
        return block.reshape(WIDTH * count, 256)

    iota_p = lax.broadcasted_iota(jnp.int32, (PR, NP), 0)
    iota_a = lax.broadcasted_iota(jnp.int32, (AR, NA), 0)

    def forward(g, _):
        for k in range(GROUPS):

            @pl.when(g == k)
            def _(k=k):
                if k:
                    for o in READY[k]:
                        arrive(o)
                for o in READY[k]:
                    arrived(o)

        base = g * WIDTH
        blocks = [key_ring(base + j) for j in range(WIDTH)]
        rows_p = kind_rows(kv, base, 0)
        keys, values = rows_p[:, :128], rows_p[:, 128:]
        sp = dot_last(keys, q_all[...]) * scaling
        causal = jnp.concatenate(
            [
                jnp.where(
                    iota_p <= q_place_p - (blocks[j] * QP + hi * PR),
                    sp[j * PR : (j + 1) * PR, :NP],
                    HIDDEN,
                )
                for j in range(WIDTH)
            ],
            axis=0,
        )
        sp = jnp.concatenate([causal, sp[:, NP:]], axis=1)
        top = jnp.max(sp, axis=0, keepdims=True)
        sa, kinds = [], []
        for k in range(2):
            rows_a = kind_rows(kv, base, k + 1)
            kinds.append(rows_a)
            sk = dot_last(rows_a[:, :128], q_all[pl.ds(NP + k * NA, NA)]) * scaling
            pieces = []
            for j in range(WIDTH):
                start = blocks[j] * QA + hi * AR
                bound = jnp.minimum(q_place_a, lens[k + 1] - 1) - start
                pieces.append(jnp.where(iota_a <= bound, sk[j * AR : (j + 1) * AR], HIDDEN))
            sa.append(jnp.concatenate(pieces, axis=0))
        tops = [top[:, :NP]]
        for k in range(2):
            a, b = NP + k * NA, NP + (k + 1) * NA
            tops.append(jnp.maximum(top[:, a:b], jnp.max(sa[k], axis=0, keepdims=True)))
        top = jnp.maximum(jnp.concatenate(tops, axis=1), FLOOR)
        wp = jnp.exp(sp - top)
        dp = dot_last(values, g_all[...])
        pp[g] = wp
        dpp[g] = dp
        total = jnp.sum(wp, axis=0, keepdims=True)
        delta = jnp.sum(wp * dp, axis=0, keepdims=True)
        out = dot_first(values, wp.astype(BF16))
        totals, deltas, outs = [total[:, :NP]], [delta[:, :NP]], [out[:, :NP]]
        for k in range(2):
            a, b = NP + k * NA, NP + (k + 1) * NA
            wa = jnp.exp(sa[k] - top[:, a:b])
            da = dot_last(kinds[k][:, 128:], g_all[pl.ds(a, NA)])
            pa[g, k] = wa
            dpa[g, k] = da
            totals.append(total[:, a:b] + jnp.sum(wa, axis=0, keepdims=True))
            deltas.append(delta[:, a:b] + jnp.sum(wa * da, axis=0, keepdims=True))
            outs.append(out[:, a:b] + dot_first(kinds[k][:, 128:], wa.astype(BF16)))
        stat[g, pl.ds(0, 1)] = top
        stat[g, pl.ds(1, 1)] = jnp.concatenate(totals, axis=1)
        stat[g, pl.ds(2, 1)] = jnp.concatenate(deltas, axis=1)
        ot[g] = jnp.concatenate(outs, axis=1)
        return 0

    lax.fori_loop(0, GROUPS, forward, 0)

    def merge(ref, count):
        top = ref[0, pl.ds(0, 1)]
        for i in range(1, count):
            top = jnp.maximum(top, ref[i, pl.ds(0, 1)])
        factors = [jnp.exp(ref[i, pl.ds(0, 1)] - top) for i in range(count)]
        total = sum(f * ref[i, pl.ds(1, 1)] for i, f in enumerate(factors))
        delta = sum(f * ref[i, pl.ds(2, 1)] for i, f in enumerate(factors))
        return top, total, delta, factors

    top, total, delta, factors = merge(stat, GROUPS)
    st[0, pl.ds(0, 1)] = top
    st[0, pl.ds(1, 1)] = total
    st[0, pl.ds(2, 1)] = delta
    sends_st = [
        remote(st.at[0], st.at[d], st_s.at[d], st_r.at[d], across(d, c)) for d in (1, 2, 3)
    ]
    for d in (1, 0, 2):
        sends_st[d].start()
    ot[0] = sum(f * ot[i] for i, f in enumerate(factors))
    dqt[...] = jnp.zeros_like(dqt)
    for copy in sends_st:
        copy.wait_recv()
    all_top, total, delta, _ = merge(st, 4)
    delta = delta / total
    scale_own = jnp.exp(top - all_top) / total
    for i in range(GROUPS):
        stat[i, pl.ds(3, 1)] = jnp.exp(stat[i, pl.ds(0, 1)] - all_top) / total

    def pass_on(o):
        mine = slot_of(o, c)
        return remote(sib_out.at[o], sib_in.at[o], sib_s.at[o], sib_r.at[o], sibling)

    def offer(o):
        def act():
            sib_out[o] = part[slot_of(o, 1 - c)].astype(BF16)
            pass_on(o).start()

        if o == 8:
            pl.when(c == 1)(act)
        else:
            act()

    def up(o):
        return remote(
            rs_out.at[o], rs_in.at[o], rs_s.at[o], rs_r.at[o], ring(-s * (o - REDUCE[o]))
        )

    def send_up(o):
        def act():
            pass_on(o).wait_recv()
            value = part[slot_of(o, c)] + sib_in[o].astype(F32)
            if o < 8:
                for o2 in children(REDUCE, o):
                    if o2 < 8:
                        up(o2).wait_recv()
                        value = value + rs_in[o2].astype(F32)
            part[slot_of(o, c)] = value
            if 8 in children(REDUCE, o):

                @pl.when(c == 0)
                def _():
                    up(8).wait_recv()
                    part[slot_of(o, c)] = part[slot_of(o, c)] + rs_in[8].astype(F32)

            rs_out[o] = part[slot_of(o, c)].astype(BF16)
            up(o).start()

        guard(o, act)

    def backward(i, _):
        g = GROUPS - 1 - i
        base = g * WIDTH
        rows_p = kind_rows(kv, base, 0)
        keys = rows_p[:, :128]
        factor = stat[g, pl.ds(3, 1)]
        w = pp[g] * factor
        ds = (w * (dpp[g] - delta)).astype(BF16)
        part[pl.ds(base, WIDTH), pl.ds(0, PR), pl.ds(0, 128)] = dot(ds, q_all[...]).reshape(
            WIDTH, PR, 128
        )
        part[pl.ds(base, WIDTH), pl.ds(0, PR), pl.ds(128, 128)] = dot(
            w.astype(BF16), g_all[...]
        ).reshape(WIDTH, PR, 128)
        dq = dot_first(keys, ds)
        dqs = [dq[:, :NP]]
        for k in range(2):
            a, b = NP + k * NA, NP + (k + 1) * NA
            rows_a = kind_rows(kv, base, k + 1)
            w = pa[g, k] * factor[:, a:b]
            ds = (w * (dpa[g, k] - delta[:, a:b])).astype(BF16)
            where = pl.ds(PR + k * AR, AR)
            part[pl.ds(base, WIDTH), where, pl.ds(0, 128)] = dot(
                ds, q_all[pl.ds(a, NA)]
            ).reshape(WIDTH, AR, 128)
            part[pl.ds(base, WIDTH), where, pl.ds(128, 128)] = dot(
                w.astype(BF16), g_all[pl.ds(a, NA)]
            ).reshape(WIDTH, AR, 128)
            dqs.append(dq[:, a:b] + dot_first(rows_a[:, :128], ds))
        dqt[...] += jnp.concatenate(dqs, axis=1)
        for k in range(GROUPS):

            @pl.when(i == k)
            def _(k=k):
                for o in DONE[k]:
                    offer(o)
                if k:
                    for o in DONE[k - 1]:
                        if not children(REDUCE, o):
                            send_up(o)

        return 0

    lax.fori_loop(0, GROUPS, backward, 0)
    for o in DONE[GROUPS - 1]:
        if not children(REDUCE, o):
            send_up(o)

    backs = []
    for j, whole in enumerate((ot[0] * scale_own, dqt[...])):
        rows = whole.T
        for d in range(4):
            for start, count, at in (
                (d * QP, QP, 0),
                (NP + d * QA, QA, QP),
                (NP + NA + d * QA, QA, QP + QA),
            ):
                piece = rows[start : start + count]
                own_f[j, d, pl.ds(at, count)] = piece
                osend[j, d, pl.ds(at, count)] = piece.astype(BF16)
        for d in (2, 1, 3):
            theirs_x = lax.rem(x + 4 - d, 4)
            back = remote(
                osend.at[j, theirs_x], orecv.at[j, d], o_s.at[j, d], o_r.at[j, d], across(-d, c)
            )
            back.start()
            backs.append(back)

    for o in sorted(REDUCE, reverse=True):
        if children(REDUCE, o):
            send_up(o)

    for back in backs:
        back.wait_recv()
    place = blk * QA + lax.broadcasted_iota(jnp.int32, (QA, 128), 0)
    for j, (p_out, a_out) in enumerate(((po, ao), (pqg, aqg))):
        value = own_f[j, x]
        for d in (1, 2, 3):
            value = value + orecv[j, d].astype(F32)
        if j:
            value = value * scaling
        p_out[...] = value[:QP].astype(BF16)
        for k in range(2):
            rows = value[QP + k * QA : QP + (k + 1) * QA]
            if j == 0:
                rows = jnp.where(place < lens[k + 1], rows, 0.0)
            a_out[k] = rows.astype(BF16)

    value = part[0]
    for o in children(REDUCE, 0)[::-1]:
        up(o).wait_recv()
        value = value + rs_in[o].astype(F32)
    fin[0, c] = value.astype(BF16)
    finals = [
        remote(fin.at[0, c], fin.at[0, c], fin_s.at[0], fin_r.at[0], sibling),
        remote(fin.at[0, c], fin.at[1, c], fin_s.at[1], fin_r.at[1], across(2, c)),
        remote(fin.at[0, c], fin.at[1, c], fin_s.at[2], fin_r.at[2], across(2, 1 - c)),
    ]
    for f in finals[::-1]:
        f.start()
    for f in finals:
        f.wait_recv()
    factor = jnp.where(lax.broadcasted_iota(jnp.int32, (1, 256), 1) < 128, scaling, 1.0)
    for h in range(2):
        half = hi if h == 0 else 1 - hi
        value = ((fin[h, 0].astype(F32) + fin[h, 1].astype(F32)) * factor).astype(BF16)
        pkvg[pl.ds(pl.multiple_of(half * PR, PR), PR)] = value[:PR]
        for k in range(2):
            akvg[k, pl.ds(pl.multiple_of(half * AR, AR), AR)] = value[
                PR + k * AR : PR + (k + 1) * AR
            ]

    for copy in sends_q + sends_st + backs + finals:
        copy.wait_send()
    for o in GATHER:
        def act(o=o):
            hop(o).wait_send()
            share(o).wait_send()
            up(o).wait_send()

        guard(o, act)
        if o == 8:
            pl.when(c == 1)(lambda: pass_on(8).wait_send())
        else:
            pass_on(o).wait_send()


def body(*args):
    vmem = pl.BlockSpec(memory_space=pltpu.VMEM)
    hbm = pl.BlockSpec(memory_space=pl.ANY)
    dma = pltpu.SemaphoreType.DMA
    outs = (
        jax.ShapeDtypeStruct((QP, 128), BF16),
        jax.ShapeDtypeStruct((2, QA, 128), BF16),
        jax.ShapeDtypeStruct((QP, 128), BF16),
        jax.ShapeDtypeStruct((2, QA, 128), BF16),
        jax.ShapeDtypeStruct((QP, 256), BF16),
        jax.ShapeDtypeStruct((2, QA, 256), BF16),
    )
    return pl.pallas_call(
        kernel,
        out_shape=outs,
        in_specs=[hbm] * 6 + [pl.BlockSpec(memory_space=pltpu.SMEM)],
        out_specs=(vmem,) * 6,
        scratch_shapes=[
            pltpu.VMEM((16, BLOCK, 256), BF16),
            pltpu.VMEM((4, OWN, 256), BF16),
            pltpu.VMEM((ROWS, 128), BF16),
            pltpu.VMEM((ROWS, 128), BF16),
            pltpu.VMEM((GROUPS, WIDTH * PR, ROWS), F32),
            pltpu.VMEM((GROUPS, WIDTH * PR, ROWS), F32),
            pltpu.VMEM((GROUPS, 2, WIDTH * AR, NA), F32),
            pltpu.VMEM((GROUPS, 2, WIDTH * AR, NA), F32),
            pltpu.VMEM((GROUPS, 8, ROWS), F32),
            pltpu.VMEM((GROUPS, 128, ROWS), F32),
            pltpu.VMEM((4, 8, ROWS), F32),
            pltpu.VMEM((128, ROWS), F32),
            pltpu.VMEM((2, 4, OWN, 128), F32),
            pltpu.VMEM((2, 4, OWN, 128), BF16),
            pltpu.VMEM((2, 4, OWN, 128), BF16),
            pltpu.VMEM((16, BLOCK, 256), F32),
            pltpu.VMEM((9, BLOCK, 256), BF16),
            pltpu.VMEM((9, BLOCK, 256), BF16),
            pltpu.VMEM((9, BLOCK, 256), BF16),
            pltpu.VMEM((9, BLOCK, 256), BF16),
            pltpu.VMEM((2, 2, BLOCK, 256), BF16),
            dma((9,)),
            dma((16,)),
            dma((9,)),
            dma((9,)),
            dma((4,)),
            dma((4,)),
            dma((4,)),
            dma((4,)),
            dma((2, 4)),
            dma((2, 4)),
            dma((9,)),
            dma((9,)),
            dma((9,)),
            dma((9,)),
            dma((3,)),
            dma((3,)),
        ],
        compiler_params=pltpu.CompilerParams(
            collective_id=0, has_side_effects=True, vmem_limit_bytes=56 * 2**20
        ),
    )(*args)


def solution(mesh):
    row = P(("batch", "blk"), "resp")
    answer = P("batch", "blk", "resp")
    row_kv = P(("batch", "blk"), None)
    answer_kv = P("batch", "blk", None)
    return jax.shard_map(
        body,
        mesh=mesh,
        in_specs=(row, answer, row_kv, answer_kv, row, answer, P("batch")),
        out_specs=(row, answer, row, answer, row_kv, answer_kv),
        check_vma=False,
    )
```

```python
import functools
import math

import jax
import jax.numpy as jnp
from jax import lax
from jax.experimental import pallas as pl
from jax.experimental.pallas import tpu as pltpu
from jax.sharding import PartitionSpec as P

MESH = pl.DeviceIdType.MESH
F32 = jnp.float32
BF16 = jnp.bfloat16
HIDDEN = -1e30
FLOOR = -1e20
RING = 16
PR, AR = 48, 32
BLOCK = PR + 2 * AR
QP, QA = 96, 64
OWN = QP + 2 * QA
ROWS = 4 * OWN
NP, NA = 4 * QP, 4 * QA
PARCELS = ((0, PR), (PR, 2 * AR))
PIECES = ((0, PR), (PR, 2 * AR))
WINDOW = 2 * AR
GROUPS, WIDTH = 4, 4

GATHER = {1: 0, 3: 0, 2: 3, 4: 3, 6: 3, 5: 6, 7: 6, 8: 6}
REDUCE = {1: 0, 3: 0, 6: 0, 2: 3, 4: 3, 5: 6, 7: 6, 8: 6}
ORDER = [1, 3, 2, 4, 6, 5, 7]


def children(tree, parent):
    return sorted([o for o, p in tree.items() if p == parent], reverse=True)


SIGNED = [0] * 16
for _i, _o in enumerate(ORDER):
    SIGNED[1 + 2 * _i], SIGNED[2 + 2 * _i] = -_o, _o
SIGNED[15] = 8


def slot_of(offset, core):
    if offset == 8:
        return 15
    return 1 + 2 * ORDER.index(offset) + core


READY = [[o for o in GATHER if min(slot_of(o, 0), 15) // WIDTH == k] for k in range(GROUPS)]
DONE = READY[::-1]
RELAYS = [o for o in ORDER if children(GATHER, o)]


def dot_last(a, b):
    return lax.dot_general(a, b, (((1,), (1,)), ((), ())), preferred_element_type=F32)


def dot_first(a, b):
    return lax.dot_general(a, b, (((0,), (0,)), ((), ())), preferred_element_type=F32)


def dot(a, b):
    return jnp.dot(a, b, preferred_element_type=F32)


def kernel(
    pq, aq, pkv, akv, pg, ag, lens,
    po, ao, pqg, aqg, pkvg, akvg,
    kv, qg, q_all, g_all, pp, dpp, pa, dpa, stat, ot, st, dqt, own_f, osend, orecv,
    part, sib_out, sib_in, rs_out, rs_in, fin, own_in,
    loc, kv_r, kv_s, kv_x, qg_r, qg_s, st_r, st_s, o_r, o_s, sib_r, sib_s, rs_r, rs_s, fin_r, fin_s, own_r, own_s,
):
    blk, resp = lax.axis_index("blk"), lax.axis_index("resp")
    lo, z = blk // RING, lax.rem(blk, RING)
    hi, c = resp // 2, lax.rem(resp, 2)
    x = hi * 2 + lo
    s = 1 - 2 * c
    scaling = 1.0 / math.sqrt(128)

    def ring(step):
        return {"blk": lo * RING + lax.rem(z + step + 2 * RING, RING), "resp": resp}

    def across(step, core):
        to = lax.rem(x + step + 4, 4)
        return {"blk": lax.rem(to, 2) * RING + z, "resp": (to // 2) * 2 + core}

    sibling = {"blk": blk, "resp": hi * 2 + 1 - c}

    def remote(src, dst, send, recv, to):
        return pltpu.make_async_remote_copy(
            src_ref=src, dst_ref=dst, send_sem=send, recv_sem=recv, device_id=to, device_id_type=MESH
        )

    def guard(offset, act):
        if offset == 8:
            pl.when(c == 0)(act)
        else:
            act()

    first_p = pl.multiple_of(hi * PR, PR)
    first_a = pl.multiple_of(hi * AR, AR)
    pairs = [
        (pkv.at[pl.ds(first_p, PR)], kv.at[0, pl.ds(0, PR)]),
        (akv.at[0, pl.ds(first_a, AR)], kv.at[0, pl.ds(PR, AR)]),
        (akv.at[1, pl.ds(first_a, AR)], kv.at[0, pl.ds(PR + AR, AR)]),
    ]
    for j, (p_ref, a_ref) in enumerate(((pq, aq), (pg, ag))):
        cols = pl.ds(128 * j, 128)
        pairs.append((p_ref, qg.at[x, pl.ds(0, QP), cols]))
        pairs.append((a_ref.at[0], qg.at[x, pl.ds(QP, QA), cols]))
        pairs.append((a_ref.at[1], qg.at[x, pl.ds(QP + QA, QA), cols]))
    loads = [pltpu.make_async_copy(a, b, loc.at[i]) for i, (a, b) in enumerate(pairs)]
    for load in loads:
        load.start()

    barrier = pltpu.get_barrier_semaphore()
    steps = sorted({o - p for o, p in GATHER.items()})
    senders = [ring(-s * d) for d in steps] + [across(d, c) for d in (1, 2, 3)] + [sibling]
    for device in senders:
        pl.semaphore_signal(barrier, inc=1, device_id=device, device_id_type=MESH)
    for load in loads:
        load.wait()
    pl.semaphore_wait(barrier, len(senders))

    def rows_of(piece):
        return pl.ds(*PIECES[piece])

    def hop(o, piece):
        p = GATHER[o]
        source = 0 if p == 0 else slot_of(p, c)
        mine, rows = slot_of(o, c), pl.ds(*PARCELS[piece])
        return remote(
            kv.at[source, rows], kv.at[mine, rows], kv_s.at[piece, o], kv_r.at[piece, mine], ring(s * (o - p))
        )

    def share(o, piece):
        mine, rows = slot_of(o, c), pl.ds(*PARCELS[piece])
        return remote(kv.at[mine, rows], kv.at[mine, rows], kv_x.at[piece, o], kv_r.at[piece, mine], sibling)

    def arrive(o):
        for piece in range(len(PARCELS)):
            hop(o, piece).wait_recv()
            for o2 in children(GATHER, o):
                hop(o2, piece).start()
            if o != 8:
                share(o, piece).start()

    def theirs(o):
        other = slot_of(o, 1 - c)
        for piece in range(len(PARCELS)):
            block = kv.at[other, pl.ds(*PARCELS[piece])]
            pltpu.make_async_copy(block, block, kv_r.at[piece, other]).wait()

    sends_q = [
        remote(qg.at[x], qg.at[x], qg_s.at[d], qg_r.at[d], across(d, c)) for d in (1, 2, 3)
    ]
    for d in (1, 0, 2):
        sends_q[d].start()
    for piece in range(len(PARCELS)):
        for o in children(GATHER, 0):
            hop(o, piece).start()
    for o in RELAYS:
        arrive(o)
    for o in READY[0]:
        if o not in RELAYS:
            arrive(o)
    for copy in sends_q:
        copy.wait_recv()

    for d in range(4):
        place = ((d % 2) * RING + z) * QA + lax.broadcasted_iota(jnp.int32, (QA, 128), 0)
        q_all[pl.ds(d * QP, QP)] = qg[d, pl.ds(0, QP), pl.ds(0, 128)]
        g_all[pl.ds(d * QP, QP)] = qg[d, pl.ds(0, QP), pl.ds(128, 128)]
        for k in range(2):
            rows = pl.ds(NP + k * NA + d * QA, QA)
            q_all[rows] = qg[d, pl.ds(QP + k * QA, QA), pl.ds(0, 128)]
            masked = jnp.where(
                place < lens[k + 1], qg[d, pl.ds(QP + k * QA, QA), pl.ds(128, 128)].astype(F32), 0.0
            )
            g_all[rows] = masked.astype(BF16)

    lane = lax.broadcasted_iota(jnp.int32, (1, NP), 1)
    which = (lane >= QP).astype(jnp.int32) + (lane >= 2 * QP) + (lane >= 3 * QP)
    q_place_p = (which & 1) * (RING * QP) + z * QP + lane - which * QP
    lane = lax.broadcasted_iota(jnp.int32, (1, NA), 1)
    which = (lane >= QA).astype(jnp.int32) + (lane >= 2 * QA) + (lane >= 3 * QA)
    q_place_a = (which & 1) * (RING * QA) + z * QA + lane - which * QA

    def key_ring(slot):
        off = jnp.int32(0)
        for k in range(1, 16):
            off = jnp.where(slot == k, SIGNED[k], off)
        return lo * RING + lax.rem(z + off + RING, RING)

    def kind_rows(ref, base, k):
        start, count = (0, PR) if k == 0 else (PR + (k - 1) * AR, AR)
        block = ref[pl.ds(base, WIDTH), pl.ds(start, count), :]
        return block.reshape(WIDTH * count, 256)

    iota_p = lax.broadcasted_iota(jnp.int32, (PR, NP), 0)
    iota_a = lax.broadcasted_iota(jnp.int32, (AR, NA), 0)

    def receive(g):
        for k in range(GROUPS):

            @pl.when(g == k)
            def _(k=k):
                if k:
                    for o in READY[k]:
                        if o not in RELAYS:
                            arrive(o)
                for o in READY[k]:
                    if o != 8:
                        theirs(o)

    def attend(g):
        base = g * WIDTH
        blocks = [key_ring(base + j) for j in range(WIDTH)]
        rows_p = kind_rows(kv, base, 0)
        keys, values = rows_p[:, :128], rows_p[:, 128:]
        sp = dot_last(keys, q_all[...]) * scaling
        causal = jnp.concatenate(
            [
                jnp.where(
                    iota_p <= q_place_p - (blocks[j] * QP + hi * PR),
                    sp[j * PR : (j + 1) * PR, :NP],
                    HIDDEN,
                )
                for j in range(WIDTH)
            ],
            axis=0,
        )
        sp = jnp.concatenate([causal, sp[:, NP:]], axis=1)
        top = jnp.max(sp, axis=0, keepdims=True)
        sa, kinds = [], []
        for k in range(2):
            rows_a = kind_rows(kv, base, k + 1)
            kinds.append(rows_a)
            sk = dot_last(rows_a[:, :128], q_all[pl.ds(NP + k * NA, NA)]) * scaling
            pieces = []
            for j in range(WIDTH):
                start = blocks[j] * QA + hi * AR
                bound = jnp.minimum(q_place_a, lens[k + 1] - 1) - start
                pieces.append(jnp.where(iota_a <= bound, sk[j * AR : (j + 1) * AR], HIDDEN))
            sa.append(jnp.concatenate(pieces, axis=0))
        tops = [top[:, :NP]]
        for k in range(2):
            a, b = NP + k * NA, NP + (k + 1) * NA
            tops.append(jnp.maximum(top[:, a:b], jnp.max(sa[k], axis=0, keepdims=True)))
        top = jnp.maximum(jnp.concatenate(tops, axis=1), FLOOR)
        wp = jnp.exp(sp - top)
        dp = dot_last(values, g_all[...])
        pp[g] = wp
        dpp[g] = dp
        total = jnp.sum(wp, axis=0, keepdims=True)
        delta = jnp.sum(wp * dp, axis=0, keepdims=True)
        out = dot_first(values, wp.astype(BF16))
        totals, deltas, outs = [total[:, :NP]], [delta[:, :NP]], [out[:, :NP]]
        for k in range(2):
            a, b = NP + k * NA, NP + (k + 1) * NA
            wa = jnp.exp(sa[k] - top[:, a:b])
            da = dot_last(kinds[k][:, 128:], g_all[pl.ds(a, NA)])
            pa[g, k] = wa
            dpa[g, k] = da
            totals.append(total[:, a:b] + jnp.sum(wa, axis=0, keepdims=True))
            deltas.append(delta[:, a:b] + jnp.sum(wa * da, axis=0, keepdims=True))
            outs.append(out[:, a:b] + dot_first(kinds[k][:, 128:], wa.astype(BF16)))
        stat[g, pl.ds(0, 1)] = top
        stat[g, pl.ds(1, 1)] = jnp.concatenate(totals, axis=1)
        stat[g, pl.ds(2, 1)] = jnp.concatenate(deltas, axis=1)
        ot[g] = jnp.concatenate(outs, axis=1)

    def forward(g, _):
        receive(g)
        attend(g)
        return 0

    lax.fori_loop(0, GROUPS, forward, 0)

    def merge(parts):
        top = functools.reduce(jnp.maximum, [p[0] for p in parts])
        factors = [jnp.exp(p[0] - top) for p in parts]
        total = sum(f * p[1] for f, p in zip(factors, parts))
        delta = sum(f * p[2] for f, p in zip(factors, parts))
        return top, total, delta, factors

    top, total, delta, factors = merge(
        [[stat[i, pl.ds(k, 1)] for k in range(3)] for i in range(GROUPS)]
    )
    st[0, 0] = top
    st[0, 1] = total
    st[0, 2] = delta
    sends_st = [
        remote(st.at[0], st.at[d], st_s.at[d], st_r.at[d], across(d, c)) for d in (1, 2, 3)
    ]
    for d in (1, 0, 2):
        sends_st[d].start()
    ot[0] = sum(f * ot[i] for i, f in enumerate(factors))
    dqt[...] = jnp.zeros_like(dqt)
    for copy in sends_st:
        copy.wait_recv()
    all_top, total, delta, _ = merge([[st[d, k] for k in range(3)] for d in range(4)])
    delta = delta / total
    scale_own = jnp.exp(top - all_top) / total
    for i in range(GROUPS):
        stat[i, pl.ds(3, 1)] = jnp.exp(stat[i, pl.ds(0, 1)] - all_top) / total

    def pass_on(o):
        mine = slot_of(o, c)
        return remote(sib_out.at[o], sib_in.at[o], sib_s.at[o], sib_r.at[o], sibling)

    def offer(o):
        def act():
            sib_out[o] = part[slot_of(o, 1 - c)].astype(BF16)
            pass_on(o).start()

        if o == 8:
            pl.when(c == 1)(act)
        else:
            act()

    def up(o, piece, direction=None):
        rows = rows_of(piece)
        step = -s * (o - REDUCE[o])
        if REDUCE[o] == 0:
            to = {"blk": lo * RING + lax.rem(z + step + 2 * RING, RING), "resp": hi * 2 + piece}
        else:
            to = ring(step)
        way = c if direction is None else direction
        return remote(
            rs_out.at[o, rows], rs_in.at[way, o, rows], rs_s.at[piece, o], rs_r.at[way, piece, o], to
        )

    def send_up(o):
        def act():
            pass_on(o).wait_recv()
            mine = slot_of(o, c)
            for piece in range(2):
                rows = rows_of(piece)
                value = part[mine, rows] + sib_in[o, rows].astype(F32)
                for o2 in children(REDUCE, o):
                    if o2 < 8:
                        up(o2, piece).wait_recv()
                        value = value + rs_in[c, o2, rows].astype(F32)
                if 8 in children(REDUCE, o):
                    part[mine, rows] = value

                    @pl.when(c == 0)
                    def _(piece=piece, rows=rows):
                        up(8, piece).wait_recv()
                        part[mine, rows] = part[mine, rows] + rs_in[0, 8, rows].astype(F32)

                    value = part[mine, rows]
                rs_out[o, rows] = value.astype(BF16)
                up(o, piece).start()

        guard(o, act)

    def differentiate(g):
        base = g * WIDTH
        rows_p = kind_rows(kv, base, 0)
        keys = rows_p[:, :128]
        factor = stat[g, pl.ds(3, 1)]
        w = pp[g] * factor
        ds = (w * (dpp[g] - delta)).astype(BF16)
        part[pl.ds(base, WIDTH), pl.ds(0, PR), pl.ds(0, 128)] = dot(ds, q_all[...]).reshape(
            WIDTH, PR, 128
        )
        part[pl.ds(base, WIDTH), pl.ds(0, PR), pl.ds(128, 128)] = dot(
            w.astype(BF16), g_all[...]
        ).reshape(WIDTH, PR, 128)
        dq = dot_first(keys, ds)
        dqs = [dq[:, :NP]]
        for k in range(2):
            a, b = NP + k * NA, NP + (k + 1) * NA
            rows_a = kind_rows(kv, base, k + 1)
            w = pa[g, k] * factor[:, a:b]
            ds = (w * (dpa[g, k] - delta[:, a:b])).astype(BF16)
            where = pl.ds(PR + k * AR, AR)
            part[pl.ds(base, WIDTH), where, pl.ds(0, 128)] = dot(
                ds, q_all[pl.ds(a, NA)]
            ).reshape(WIDTH, AR, 128)
            part[pl.ds(base, WIDTH), where, pl.ds(128, 128)] = dot(
                w.astype(BF16), g_all[pl.ds(a, NA)]
            ).reshape(WIDTH, AR, 128)
            dqs.append(dq[:, a:b] + dot_first(rows_a[:, :128], ds))
        dqt[...] += jnp.concatenate(dqs, axis=1)

    def reduce(i):
        for k in range(GROUPS):

            @pl.when(i == k)
            def _(k=k):
                for o in DONE[k]:
                    offer(o)
                if k:
                    for o in DONE[k - 1]:
                        if not children(REDUCE, o):
                            send_up(o)

    def backward(i, _):
        differentiate(GROUPS - 1 - i)
        reduce(i)
        return 0

    lax.fori_loop(0, GROUPS, backward, 0)
    other = pl.multiple_of((1 - c) * PR, PR)
    swap = remote(part.at[0, pl.ds(other, WINDOW)], own_in, own_s, own_r, sibling)
    swap.start()
    for o in DONE[GROUPS - 1]:
        if not children(REDUCE, o):
            send_up(o)

    backs = []
    for j, whole in enumerate((ot[0] * scale_own, dqt[...])):
        rows = whole.T
        for d in range(4):
            for start, count, at in (
                (d * QP, QP, 0),
                (NP + d * QA, QA, QP),
                (NP + NA + d * QA, QA, QP + QA),
            ):
                piece = rows[start : start + count]
                own_f[j, d, pl.ds(at, count)] = piece
                osend[j, d, pl.ds(at, count)] = piece.astype(BF16)
        for d in (2, 1, 3):
            theirs_x = lax.rem(x + 4 - d, 4)
            back = remote(
                osend.at[j, theirs_x], orecv.at[j, d], o_s.at[j, d], o_r.at[j, d], across(-d, c)
            )
            back.start()
            backs.append(back)

    for o in sorted(REDUCE, reverse=True):
        if children(REDUCE, o):
            send_up(o)

    for back in backs:
        back.wait_recv()
    place = blk * QA + lax.broadcasted_iota(jnp.int32, (QA, 128), 0)
    for j, (p_out, a_out) in enumerate(((po, ao), (pqg, aqg))):
        value = own_f[j, x]
        for d in (1, 2, 3):
            value = value + orecv[j, d].astype(F32)
        if j:
            value = value * scaling
        p_out[...] = value[:QP].astype(BF16)
        for k in range(2):
            rows = value[QP + k * QA : QP + (k + 1) * QA]
            if j == 0:
                rows = jnp.where(place < lens[k + 1], rows, 0.0)
            a_out[k] = rows.astype(BF16)

    swap.wait_recv()
    first = pl.multiple_of(c * PR, PR)
    window = pl.ds(first, WINDOW)
    value = part[0, window] + own_in[...]
    for o in children(REDUCE, 0)[::-1]:
        for way in range(2):
            for piece in range(2):
                pl.when(c == piece)(lambda: up(o, piece, way).wait_recv())
            value = value + rs_in[way, o, window].astype(F32)
    factor = jnp.where(lax.broadcasted_iota(jnp.int32, (1, 256), 1) < 128, scaling, 1.0)
    fin[0, c] = (value * factor).astype(BF16)
    finals = [
        remote(fin.at[0, c], fin.at[0, c], fin_s.at[0], fin_r.at[0, 0], sibling),
        remote(fin.at[0, c], fin.at[1, c], fin_s.at[1], fin_r.at[1, c], across(2, c)),
        remote(fin.at[0, c], fin.at[1, c], fin_s.at[2], fin_r.at[1, c], across(2, 1 - c)),
    ]
    for f in finals[::-1]:
        f.start()
    for h in range(2):
        half = hi if h == 0 else 1 - hi
        if h == 0:
            finals[0].wait_recv()
        else:
            for core in range(2):
                block = fin.at[1, core]
                pltpu.make_async_copy(block, block, fin_r.at[1, core]).wait()
        pkvg[pl.ds(pl.multiple_of(half * PR, PR), PR)] = fin[h, 0, pl.ds(0, PR)]
        for k in range(2):
            akvg[k, pl.ds(pl.multiple_of(half * AR, AR), AR)] = fin[h, 1, pl.ds(k * AR, AR)]

    for copy in sends_q + sends_st + backs + finals + [swap]:
        copy.wait_send()
    for o in GATHER:
        for piece in range(len(PARCELS)):
            hop(o, piece).wait_send()
            if o != 8:
                share(o, piece).wait_send()

        def sent(o=o):
            for piece in range(2):
                up(o, piece).wait_send()

        guard(o, sent)
        if o == 8:
            pl.when(c == 1)(lambda: pass_on(8).wait_send())
        else:
            pass_on(o).wait_send()


def place(*refs):
    for source, target in zip(refs[:6], refs[6:]):
        target[...] = source[...]


def body(*args):
    vmem = pl.BlockSpec(memory_space=pltpu.VMEM)
    hbm = pl.BlockSpec(memory_space=pl.ANY)
    dma = pltpu.SemaphoreType.DMA
    outs = (
        jax.ShapeDtypeStruct((QP, 128), BF16),
        jax.ShapeDtypeStruct((2, QA, 128), BF16),
        jax.ShapeDtypeStruct((QP, 128), BF16),
        jax.ShapeDtypeStruct((2, QA, 128), BF16),
        jax.ShapeDtypeStruct((QP, 256), BF16),
        jax.ShapeDtypeStruct((2, QA, 256), BF16),
    )
    results = pl.pallas_call(
        kernel,
        out_shape=outs,
        in_specs=[hbm] * 6 + [pl.BlockSpec(memory_space=pltpu.SMEM)],
        out_specs=(vmem,) * 6,
        scratch_shapes=[
            pltpu.VMEM((16, BLOCK, 256), BF16),
            pltpu.VMEM((4, OWN, 256), BF16),
            pltpu.VMEM((ROWS, 128), BF16),
            pltpu.VMEM((ROWS, 128), BF16),
            pltpu.VMEM((GROUPS, WIDTH * PR, ROWS), F32),
            pltpu.VMEM((GROUPS, WIDTH * PR, ROWS), F32),
            pltpu.VMEM((GROUPS, 2, WIDTH * AR, NA), F32),
            pltpu.VMEM((GROUPS, 2, WIDTH * AR, NA), F32),
            pltpu.VMEM((GROUPS, 8, ROWS), F32),
            pltpu.VMEM((GROUPS, 128, ROWS), F32),
            pltpu.VMEM((4, 3, 1, ROWS), F32),
            pltpu.VMEM((128, ROWS), F32),
            pltpu.VMEM((2, 4, OWN, 128), F32),
            pltpu.VMEM((2, 4, OWN, 128), BF16),
            pltpu.VMEM((2, 4, OWN, 128), BF16),
            pltpu.VMEM((16, BLOCK, 256), F32),
            pltpu.VMEM((9, BLOCK, 256), BF16),
            pltpu.VMEM((9, BLOCK, 256), BF16),
            pltpu.VMEM((9, BLOCK, 256), BF16),
            pltpu.VMEM((2, 9, BLOCK, 256), BF16),
            pltpu.VMEM((2, 2, WINDOW, 256), BF16),
            pltpu.VMEM((WINDOW, 256), F32),
            dma((9,)),
            dma((len(PARCELS), 16)),
            dma((len(PARCELS), 9)),
            dma((len(PARCELS), 9)),
            dma((4,)),
            dma((4,)),
            dma((4,)),
            dma((4,)),
            dma((2, 4)),
            dma((2, 4)),
            dma((9,)),
            dma((9,)),
            dma((2, 2, 9)),
            dma((2, 9)),
            dma((2, 2)),
            dma((3,)),
            dma(()),
            dma(()),
        ],
        compiler_params=pltpu.CompilerParams(
            collective_id=0, has_side_effects=True, vmem_limit_bytes=56 * 2**20
        ),
    )(*args)
    return pl.pallas_call(
        place,
        out_shape=outs,
        in_specs=[vmem] * 6,
        out_specs=(vmem,) * 6,
        compiler_params=pltpu.CompilerParams(vmem_limit_bytes=56 * 2**20),
    )(*results)


def solution(mesh):
    row = P(("batch", "blk"), "resp")
    answer = P("batch", "blk", "resp")
    row_kv = P(("batch", "blk"), None)
    answer_kv = P("batch", "blk", None)
    return jax.shard_map(
        body,
        mesh=mesh,
        in_specs=(row, answer, row_kv, answer_kv, row, answer, P("batch")),
        out_specs=(row, answer, row, answer, row_kv, answer_kv),
        check_vma=False,
    )
```

```python
import functools
import math

import jax
import jax.numpy as jnp
from jax import lax
from jax.experimental import pallas as pl
from jax.experimental.pallas import tpu as pltpu
from jax.sharding import PartitionSpec as P

MESH = pl.DeviceIdType.MESH
F32 = jnp.float32
BF16 = jnp.bfloat16
HIDDEN = -1e30
FLOOR = -1e20
RING = 16
PR, AR = 48, 32
BLOCK = PR + 2 * AR
QP, QA = 96, 64
OWN = QP + 2 * QA
ROWS = 4 * OWN
NP, NA = 4 * QP, 4 * QA
PARCELS = ((0, PR), (PR, 2 * AR))
PIECES = ((0, PR), (PR, 2 * AR))
FINISHER = (0, 1)
WINDOW = 2 * AR
GROUPS, WIDTH = 4, 4

GATHER = {1: 0, 3: 0, 2: 3, 4: 3, 6: 3, 5: 6, 7: 6, 8: 6}
REDUCE = {1: 0, 3: 0, 6: 0, 2: 3, 4: 3, 5: 6, 7: 6, 8: 6}
ORDER = [1, 3, 2, 4, 6, 5, 7]


def children(tree, parent):
    return sorted([o for o, p in tree.items() if p == parent], reverse=True)


SIGNED = [0] * 16
for _i, _o in enumerate(ORDER):
    SIGNED[1 + 2 * _i], SIGNED[2 + 2 * _i] = -_o, _o
SIGNED[15] = 8


def slot_of(offset, core):
    if offset == 8:
        return 15
    return 1 + 2 * ORDER.index(offset) + core


READY = [[o for o in GATHER if min(slot_of(o, 0), 15) // WIDTH == k] for k in range(GROUPS)]
DONE = READY[::-1]
TAKEN = [[], [2, 4], [5, 7], [8]]
RELAYS = [o for o in ORDER if children(GATHER, o)]


def dot_last(a, b):
    return lax.dot_general(a, b, (((1,), (1,)), ((), ())), preferred_element_type=F32)


def dot_first(a, b):
    return lax.dot_general(a, b, (((0,), (0,)), ((), ())), preferred_element_type=F32)


def dot(a, b):
    return jnp.dot(a, b, preferred_element_type=F32)


def kernel(
    pq, aq, pkv, akv, pg, ag, lens,
    packed,
    kv, qg, q_all, g_all, pp, dpp, pa, dpa, stat, ot, st, dqt, own_f, osend, orecv,
    part, sib_out, sib_in, rs_out, rs_in, fin, own_in,
    loc, kv_r, kv_s, kv_x, qg_r, qg_s, st_r, st_s, o_r, o_s, sib_r, sib_s, rs_r, rs_s, fin_r, fin_s, own_r, own_s,
):
    blk, resp = lax.axis_index("blk"), lax.axis_index("resp")
    lo, z = blk // RING, lax.rem(blk, RING)
    hi, c = resp // 2, lax.rem(resp, 2)
    x = hi * 2 + lo
    s = 1 - 2 * c
    scaling = 1.0 / math.sqrt(128)

    def ring(step):
        return {"blk": lo * RING + lax.rem(z + step + 2 * RING, RING), "resp": resp}

    def across(step, core):
        to = lax.rem(x + step + 4, 4)
        return {"blk": lax.rem(to, 2) * RING + z, "resp": (to // 2) * 2 + core}

    sibling = {"blk": blk, "resp": hi * 2 + 1 - c}

    def remote(src, dst, send, recv, to):
        return pltpu.make_async_remote_copy(
            src_ref=src, dst_ref=dst, send_sem=send, recv_sem=recv, device_id=to, device_id_type=MESH
        )

    def guard(offset, act):
        if offset == 8:
            pl.when(c == 0)(act)
        else:
            act()

    first_p = pl.multiple_of(hi * PR, PR)
    first_a = pl.multiple_of(hi * AR, AR)
    pairs = [
        (pkv.at[pl.ds(first_p, PR)], kv.at[0, pl.ds(0, PR)]),
        (akv.at[0, pl.ds(first_a, AR)], kv.at[0, pl.ds(PR, AR)]),
        (akv.at[1, pl.ds(first_a, AR)], kv.at[0, pl.ds(PR + AR, AR)]),
    ]
    for j, (p_ref, a_ref) in enumerate(((pq, aq), (pg, ag))):
        cols = pl.ds(128 * j, 128)
        pairs.append((p_ref, qg.at[x, pl.ds(0, QP), cols]))
        pairs.append((a_ref.at[0], qg.at[x, pl.ds(QP, QA), cols]))
        pairs.append((a_ref.at[1], qg.at[x, pl.ds(QP + QA, QA), cols]))
    loads = [pltpu.make_async_copy(a, b, loc.at[i]) for i, (a, b) in enumerate(pairs)]
    barrier = pltpu.get_barrier_semaphore()
    steps = sorted({o - p for o, p in GATHER.items()})
    senders = [ring(-s * d) for d in steps] + [across(d, c) for d in (1, 2, 3)] + [sibling]
    for device in senders:
        pl.semaphore_signal(barrier, inc=1, device_id=device, device_id_type=MESH)
    for load in loads:
        load.start()
    for load in loads:
        load.wait()
    pl.semaphore_wait(barrier, len(senders))

    def rows_of(piece):
        return pl.ds(*PIECES[piece])

    def hop(o, piece):
        p = GATHER[o]
        source = 0 if p == 0 else slot_of(p, c)
        mine, rows = slot_of(o, c), pl.ds(*PARCELS[piece])
        return remote(
            kv.at[source, rows], kv.at[mine, rows], kv_s.at[piece, o], kv_r.at[piece, mine], ring(s * (o - p))
        )

    def share(o, piece):
        mine, rows = slot_of(o, c), pl.ds(*PARCELS[piece])
        return remote(kv.at[mine, rows], kv.at[mine, rows], kv_x.at[piece, o], kv_r.at[piece, mine], sibling)

    def arrive(o):
        for piece in range(len(PARCELS)):
            hop(o, piece).wait_recv()
            for o2 in children(GATHER, o):
                hop(o2, piece).start()
            if o != 8:
                share(o, piece).start()

    def theirs(o):
        other = slot_of(o, 1 - c)
        for piece in range(len(PARCELS)):
            block = kv.at[other, pl.ds(*PARCELS[piece])]
            pltpu.make_async_copy(block, block, kv_r.at[piece, other]).wait()

    sends_q = [
        remote(qg.at[x], qg.at[x], qg_s.at[d], qg_r.at[d], across(d, c)) for d in (1, 2, 3)
    ]
    for d in (1, 0, 2):
        sends_q[d].start()
    for piece in range(len(PARCELS)):
        for o in children(GATHER, 0):
            hop(o, piece).start()
    for o in RELAYS:
        arrive(o)
    for o in READY[0]:
        if o not in RELAYS:
            arrive(o)
    for copy in sends_q:
        copy.wait_recv()

    for d in range(4):
        place = ((d % 2) * RING + z) * QA + lax.broadcasted_iota(jnp.int32, (QA, 128), 0)
        q_all[pl.ds(d * QP, QP)] = qg[d, pl.ds(0, QP), pl.ds(0, 128)]
        g_all[pl.ds(d * QP, QP)] = qg[d, pl.ds(0, QP), pl.ds(128, 128)]
        for k in range(2):
            rows = pl.ds(NP + k * NA + d * QA, QA)
            q_all[rows] = qg[d, pl.ds(QP + k * QA, QA), pl.ds(0, 128)]
            masked = jnp.where(
                place < lens[k + 1], qg[d, pl.ds(QP + k * QA, QA), pl.ds(128, 128)].astype(F32), 0.0
            )
            g_all[rows] = masked.astype(BF16)

    lane = lax.broadcasted_iota(jnp.int32, (1, NP), 1)
    which = (lane >= QP).astype(jnp.int32) + (lane >= 2 * QP) + (lane >= 3 * QP)
    q_place_p = (which & 1) * (RING * QP) + z * QP + lane - which * QP
    lane = lax.broadcasted_iota(jnp.int32, (1, NA), 1)
    which = (lane >= QA).astype(jnp.int32) + (lane >= 2 * QA) + (lane >= 3 * QA)
    q_place_a = (which & 1) * (RING * QA) + z * QA + lane - which * QA

    def key_ring(slot):
        off = jnp.int32(0)
        for k in range(1, 16):
            off = jnp.where(slot == k, SIGNED[k], off)
        return lo * RING + lax.rem(z + off + RING, RING)

    def kind_rows(ref, base, k):
        start, count = (0, PR) if k == 0 else (PR + (k - 1) * AR, AR)
        block = ref[pl.ds(base, WIDTH), pl.ds(start, count), :]
        return block.reshape(WIDTH * count, 256)

    iota_p = lax.broadcasted_iota(jnp.int32, (PR, NP), 0)
    iota_a = lax.broadcasted_iota(jnp.int32, (AR, NA), 0)

    def receive(g):
        for k in range(GROUPS):

            @pl.when(g == k)
            def _(k=k):
                if k:
                    for o in TAKEN[k]:
                        arrive(o)
                for o in READY[k]:
                    if o != 8:
                        theirs(o)

    def attend(g):
        base = g * WIDTH
        blocks = [key_ring(base + j) for j in range(WIDTH)]
        rows_p = kind_rows(kv, base, 0)
        keys, values = rows_p[:, :128], rows_p[:, 128:]
        sp = dot_last(keys, q_all[...]) * scaling
        causal = jnp.concatenate(
            [
                jnp.where(
                    iota_p <= q_place_p - (blocks[j] * QP + hi * PR),
                    sp[j * PR : (j + 1) * PR, :NP],
                    HIDDEN,
                )
                for j in range(WIDTH)
            ],
            axis=0,
        )
        sp = jnp.concatenate([causal, sp[:, NP:]], axis=1)
        top = jnp.max(sp, axis=0, keepdims=True)
        sa, kinds = [], []
        for k in range(2):
            rows_a = kind_rows(kv, base, k + 1)
            kinds.append(rows_a)
            sk = dot_last(rows_a[:, :128], q_all[pl.ds(NP + k * NA, NA)]) * scaling
            pieces = []
            for j in range(WIDTH):
                start = blocks[j] * QA + hi * AR
                bound = jnp.minimum(q_place_a, lens[k + 1] - 1) - start
                pieces.append(jnp.where(iota_a <= bound, sk[j * AR : (j + 1) * AR], HIDDEN))
            sa.append(jnp.concatenate(pieces, axis=0))
        tops = [top[:, :NP]]
        for k in range(2):
            a, b = NP + k * NA, NP + (k + 1) * NA
            tops.append(jnp.maximum(top[:, a:b], jnp.max(sa[k], axis=0, keepdims=True)))
        top = jnp.maximum(jnp.concatenate(tops, axis=1), FLOOR)
        wp = jnp.exp(sp - top)
        dp = dot_last(values, g_all[...])
        pp[g] = wp
        dpp[g] = dp
        total = jnp.sum(wp, axis=0, keepdims=True)
        delta = jnp.sum(wp * dp, axis=0, keepdims=True)
        out = dot_first(values, wp.astype(BF16))
        totals, deltas, outs = [total[:, :NP]], [delta[:, :NP]], [out[:, :NP]]
        for k in range(2):
            a, b = NP + k * NA, NP + (k + 1) * NA
            wa = jnp.exp(sa[k] - top[:, a:b])
            da = dot_last(kinds[k][:, 128:], g_all[pl.ds(a, NA)])
            pa[g, k] = wa
            dpa[g, k] = da
            totals.append(total[:, a:b] + jnp.sum(wa, axis=0, keepdims=True))
            deltas.append(delta[:, a:b] + jnp.sum(wa * da, axis=0, keepdims=True))
            outs.append(out[:, a:b] + dot_first(kinds[k][:, 128:], wa.astype(BF16)))
        stat[g, pl.ds(0, 1)] = top
        stat[g, pl.ds(1, 1)] = jnp.concatenate(totals, axis=1)
        stat[g, pl.ds(2, 1)] = jnp.concatenate(deltas, axis=1)
        ot[g] = jnp.concatenate(outs, axis=1)

    def forward(g, _):
        receive(g)
        attend(g)
        return 0

    lax.fori_loop(0, GROUPS, forward, 0)

    def merge(parts):
        top = functools.reduce(jnp.maximum, [p[0] for p in parts])
        factors = [jnp.exp(p[0] - top) for p in parts]
        total = sum(f * p[1] for f, p in zip(factors, parts))
        delta = sum(f * p[2] for f, p in zip(factors, parts))
        return top, total, delta, factors

    top, total, delta, factors = merge(
        [[stat[i, pl.ds(k, 1)] for k in range(3)] for i in range(GROUPS)]
    )
    st[0, 0] = top
    st[0, 1] = total
    st[0, 2] = delta
    sends_st = [
        remote(st.at[0], st.at[d], st_s.at[d], st_r.at[d], across(d, c)) for d in (1, 2, 3)
    ]
    for d in (1, 0, 2):
        sends_st[d].start()
    ot[0] = sum(f * ot[i] for i, f in enumerate(factors))
    dqt[...] = jnp.zeros_like(dqt)
    for copy in sends_st:
        copy.wait_recv()
    all_top, total, delta, _ = merge([[st[d, k] for k in range(3)] for d in range(4)])
    delta = delta / total
    scale_own = jnp.exp(top - all_top) / total
    for i in range(GROUPS):
        stat[i, pl.ds(3, 1)] = jnp.exp(stat[i, pl.ds(0, 1)] - all_top) / total

    def pass_on(o):
        mine = slot_of(o, c)
        return remote(sib_out.at[o], sib_in.at[o], sib_s.at[o], sib_r.at[o], sibling)

    def offer(o):
        def act():
            sib_out[o] = part[slot_of(o, 1 - c)].astype(BF16)
            pass_on(o).start()

        if o == 8:
            pl.when(c == 1)(act)
        else:
            act()

    def up(o, piece, direction=None):
        rows = rows_of(piece)
        step = -s * (o - REDUCE[o])
        if REDUCE[o] == 0:
            to = {"blk": lo * RING + lax.rem(z + step + 2 * RING, RING), "resp": hi * 2 + FINISHER[piece]}
        else:
            to = ring(step)
        way = c if direction is None else direction
        return remote(
            rs_out.at[o, rows], rs_in.at[way, o, rows], rs_s.at[piece, o], rs_r.at[way, piece, o], to
        )

    def send_up(o):
        def act():
            pass_on(o).wait_recv()
            mine = slot_of(o, c)
            for piece in range(len(PIECES)):
                rows = rows_of(piece)
                value = part[mine, rows] + sib_in[o, rows].astype(F32)
                for o2 in children(REDUCE, o):
                    if o2 < 8:
                        up(o2, piece).wait_recv()
                        value = value + rs_in[c, o2, rows].astype(F32)
                if 8 in children(REDUCE, o):
                    part[mine, rows] = value

                    @pl.when(c == 0)
                    def _(piece=piece, rows=rows):
                        up(8, piece).wait_recv()
                        part[mine, rows] = part[mine, rows] + rs_in[0, 8, rows].astype(F32)

                    value = part[mine, rows]
                rs_out[o, rows] = value.astype(BF16)
                up(o, piece).start()

        guard(o, act)

    def differentiate(g):
        base = g * WIDTH
        rows_p = kind_rows(kv, base, 0)
        keys = rows_p[:, :128]
        factor = stat[g, pl.ds(3, 1)]
        w = pp[g] * factor
        ds = (w * (dpp[g] - delta)).astype(BF16)
        part[pl.ds(base, WIDTH), pl.ds(0, PR), pl.ds(0, 128)] = dot(ds, q_all[...]).reshape(
            WIDTH, PR, 128
        )
        part[pl.ds(base, WIDTH), pl.ds(0, PR), pl.ds(128, 128)] = dot(
            w.astype(BF16), g_all[...]
        ).reshape(WIDTH, PR, 128)
        dq = dot_first(keys, ds)
        dqs = [dq[:, :NP]]
        for k in range(2):
            a, b = NP + k * NA, NP + (k + 1) * NA
            rows_a = kind_rows(kv, base, k + 1)
            w = pa[g, k] * factor[:, a:b]
            ds = (w * (dpa[g, k] - delta[:, a:b])).astype(BF16)
            where = pl.ds(PR + k * AR, AR)
            part[pl.ds(base, WIDTH), where, pl.ds(0, 128)] = dot(
                ds, q_all[pl.ds(a, NA)]
            ).reshape(WIDTH, AR, 128)
            part[pl.ds(base, WIDTH), where, pl.ds(128, 128)] = dot(
                w.astype(BF16), g_all[pl.ds(a, NA)]
            ).reshape(WIDTH, AR, 128)
            dqs.append(dq[:, a:b] + dot_first(rows_a[:, :128], ds))
        dqt[...] += jnp.concatenate(dqs, axis=1)

    def reduce(i):
        for k in range(GROUPS):

            @pl.when(i == k)
            def _(k=k):
                for o in DONE[k]:
                    offer(o)
                if k:
                    for o in DONE[k - 1]:
                        if not children(REDUCE, o):
                            send_up(o)

    def backward(i, _):
        differentiate(GROUPS - 1 - i)
        reduce(i)
        return 0

    lax.fori_loop(0, GROUPS, backward, 0)
    other = pl.multiple_of((1 - c) * PR, PR)
    swap = remote(part.at[0, pl.ds(other, WINDOW)], own_in, own_s, own_r, sibling)
    swap.start()
    for o in DONE[GROUPS - 1]:
        if not children(REDUCE, o):
            send_up(o)

    backs = []
    for j, whole in enumerate((ot[0] * scale_own, dqt[...])):
        rows = whole.T
        for d in range(4):
            for start, count, at in (
                (d * QP, QP, 0),
                (NP + d * QA, QA, QP),
                (NP + NA + d * QA, QA, QP + QA),
            ):
                piece = rows[start : start + count]
                own_f[j, d, pl.ds(at, count)] = piece
                osend[j, d, pl.ds(at, count)] = piece.astype(BF16)
        for d in (2, 1, 3):
            theirs_x = lax.rem(x + 4 - d, 4)
            back = remote(
                osend.at[j, theirs_x], orecv.at[j, d], o_s.at[j, d], o_r.at[j, d], across(-d, c)
            )
            back.start()
            backs.append(back)

    def early(o):
        return lax.rem(z - s * o + RING, RING) < 7

    for o in sorted(REDUCE, reverse=True):
        if children(REDUCE, o):
            pl.when(early(o))(lambda o=o: send_up(o))

    for back in backs:
        back.wait_recv()
    place = blk * QA + lax.broadcasted_iota(jnp.int32, (QA, 128), 0)
    for j in range(2):
        cols = pl.ds(128 * j, 128)
        value = own_f[j, x]
        for d in (1, 2, 3):
            value = value + orecv[j, d].astype(F32)
        if j:
            value = value * scaling
        packed[pl.ds(0, QP), cols] = value[:QP].astype(BF16)
        for k in range(2):
            rows = value[QP + k * QA : QP + (k + 1) * QA]
            if j == 0:
                rows = jnp.where(place < lens[k + 1], rows, 0.0)
            packed[pl.ds(QP + k * QA, QA), cols] = rows.astype(BF16)

    for o in sorted(REDUCE, reverse=True):
        if children(REDUCE, o):
            pl.when(jnp.logical_not(early(o)))(lambda o=o: send_up(o))

    swap.wait_recv()
    first = pl.multiple_of(c * PR, PR)
    window = pl.ds(first, WINDOW)
    value = part[0, window] + own_in[...]
    for o in children(REDUCE, 0)[::-1]:
        for way in range(2):
            for piece, core in enumerate(FINISHER):
                pl.when(c == core)(lambda: up(o, piece, way).wait_recv())
            value = value + rs_in[way, o, window].astype(F32)
    factor = jnp.where(lax.broadcasted_iota(jnp.int32, (1, 256), 1) < 128, scaling, 1.0)
    fin[0, c] = (value * factor).astype(BF16)
    finals = [
        remote(fin.at[0, c], fin.at[0, c], fin_s.at[0], fin_r.at[0, 0], sibling),
        remote(fin.at[0, c], fin.at[1, c], fin_s.at[1], fin_r.at[1, c], across(2, c)),
        remote(fin.at[0, c], fin.at[1, c], fin_s.at[2], fin_r.at[1, c], across(2, 1 - c)),
    ]
    for f in finals[::-1]:
        f.start()
    for h in range(2):
        half = hi if h == 0 else 1 - hi
        if h == 0:
            finals[0].wait_recv()
        else:
            for core in range(2):
                block = fin.at[1, core]
                pltpu.make_async_copy(block, block, fin_r.at[1, core]).wait()
        cols = pl.ds(256, 256)
        packed[pl.ds(pl.multiple_of(half * PR, PR), PR), cols] = fin[h, 0, pl.ds(0, PR)]
        for k in range(2):
            packed[pl.ds(pl.multiple_of(QP + k * QA + half * AR, AR), AR), cols] = fin[h, 1, pl.ds(k * AR, AR)]

    for copy in sends_q + sends_st + backs + finals + [swap]:
        copy.wait_send()
    for o in GATHER:
        for piece in range(len(PARCELS)):
            hop(o, piece).wait_send()
            if o != 8:
                share(o, piece).wait_send()

        def sent(o=o):
            for piece in range(len(PIECES)):
                up(o, piece).wait_send()

        guard(o, sent)
        if o == 8:
            pl.when(c == 1)(lambda: pass_on(8).wait_send())
        else:
            pass_on(o).wait_send()


def place(packed, *refs):
    for j in range(3):
        cols = pl.ds(128 * j, 128 if j < 2 else 256)
        refs[2 * j][...] = packed[pl.ds(0, QP), cols]
        for k in range(2):
            refs[2 * j + 1][k] = packed[pl.ds(QP + k * QA, QA), cols]


def body(*args):
    vmem = pl.BlockSpec(memory_space=pltpu.VMEM)
    hbm = pl.BlockSpec(memory_space=pl.ANY)
    dma = pltpu.SemaphoreType.DMA
    outs = (
        jax.ShapeDtypeStruct((QP, 128), BF16),
        jax.ShapeDtypeStruct((2, QA, 128), BF16),
        jax.ShapeDtypeStruct((QP, 128), BF16),
        jax.ShapeDtypeStruct((2, QA, 128), BF16),
        jax.ShapeDtypeStruct((QP, 256), BF16),
        jax.ShapeDtypeStruct((2, QA, 256), BF16),
    )
    results = pl.pallas_call(
        kernel,
        out_shape=jax.ShapeDtypeStruct((OWN, 512), BF16),
        in_specs=[hbm] * 6 + [pl.BlockSpec(memory_space=pltpu.SMEM)],
        out_specs=vmem,
        scratch_shapes=[
            pltpu.VMEM((16, BLOCK, 256), BF16),
            pltpu.VMEM((4, OWN, 256), BF16),
            pltpu.VMEM((ROWS, 128), BF16),
            pltpu.VMEM((ROWS, 128), BF16),
            pltpu.VMEM((GROUPS, WIDTH * PR, ROWS), F32),
            pltpu.VMEM((GROUPS, WIDTH * PR, ROWS), F32),
            pltpu.VMEM((GROUPS, 2, WIDTH * AR, NA), F32),
            pltpu.VMEM((GROUPS, 2, WIDTH * AR, NA), F32),
            pltpu.VMEM((GROUPS, 8, ROWS), F32),
            pltpu.VMEM((GROUPS, 128, ROWS), F32),
            pltpu.VMEM((4, 3, 1, ROWS), F32),
            pltpu.VMEM((128, ROWS), F32),
            pltpu.VMEM((2, 4, OWN, 128), F32),
            pltpu.VMEM((2, 4, OWN, 128), BF16),
            pltpu.VMEM((2, 4, OWN, 128), BF16),
            pltpu.VMEM((16, BLOCK, 256), F32),
            pltpu.VMEM((9, BLOCK, 256), BF16),
            pltpu.VMEM((9, BLOCK, 256), BF16),
            pltpu.VMEM((9, BLOCK, 256), BF16),
            pltpu.VMEM((2, 9, BLOCK, 256), BF16),
            pltpu.VMEM((2, 2, WINDOW, 256), BF16),
            pltpu.VMEM((WINDOW, 256), F32),
            dma((9,)),
            dma((len(PARCELS), 16)),
            dma((len(PARCELS), 9)),
            dma((len(PARCELS), 9)),
            dma((4,)),
            dma((4,)),
            dma((4,)),
            dma((4,)),
            dma((2, 4)),
            dma((2, 4)),
            dma((9,)),
            dma((9,)),
            dma((2, len(PIECES), 9)),
            dma((len(PIECES), 9)),
            dma((2, 2)),
            dma((3,)),
            dma(()),
            dma(()),
        ],
        compiler_params=pltpu.CompilerParams(
            collective_id=0, has_side_effects=True, vmem_limit_bytes=56 * 2**20
        ),
    )(*args)
    return pl.pallas_call(
        place,
        out_shape=outs,
        in_specs=[vmem],
        out_specs=(vmem,) * 6,
        compiler_params=pltpu.CompilerParams(vmem_limit_bytes=56 * 2**20),
    )(results)


def solution(mesh):
    row = P(("batch", "blk"), "resp")
    answer = P("batch", "blk", "resp")
    row_kv = P(("batch", "blk"), None)
    answer_kv = P("batch", "blk", None)
    return jax.shard_map(
        body,
        mesh=mesh,
        in_specs=(row, answer, row_kv, answer_kv, row, answer, P("batch")),
        out_specs=(row, answer, row, answer, row_kv, answer_kv),
        check_vma=False,
    )
```

```python
import functools
import math

import jax
import jax.numpy as jnp
from jax import lax
from jax.experimental import pallas as pl
from jax.experimental.pallas import tpu as pltpu
from jax.sharding import PartitionSpec as P

MESH = pl.DeviceIdType.MESH
F32 = jnp.float32
BF16 = jnp.bfloat16
HIDDEN = -1e30
FLOOR = -1e20
RING = 16
PR, AR = 48, 32
BLOCK = PR + 2 * AR
QP, QA = 96, 64
OWN = QP + 2 * QA
ROWS = 4 * OWN
NP, NA = 4 * QP, 4 * QA
PARCELS = ((0, PR), (PR, 2 * AR))
PIECES = ((0, PR), (PR, 2 * AR))
FINISHER = (0, 1)
WINDOW = 2 * AR
GROUPS, WIDTH = 4, 4

GATHER = {1: 0, 3: 0, 2: 3, 4: 3, 6: 3, 5: 6, 7: 6, 8: 6}
REDUCE = {1: 0, 3: 0, 6: 0, 2: 3, 4: 3, 5: 6, 7: 6, 8: 6}
ORDER = [1, 3, 2, 4, 6, 5, 7]


def children(tree, parent):
    return sorted([o for o, p in tree.items() if p == parent], reverse=True)


SIGNED = [0] * 16
for _i, _o in enumerate(ORDER):
    SIGNED[1 + 2 * _i], SIGNED[2 + 2 * _i] = -_o, _o
SIGNED[15] = 8


def slot_of(offset, core):
    if offset == 8:
        return 15
    return 1 + 2 * ORDER.index(offset) + core


READY = [[o for o in GATHER if min(slot_of(o, 0), 15) // WIDTH == k] for k in range(GROUPS)]
DONE = READY[::-1]
TAKEN = [[3, 1, 6, 2, 4], [], [5, 7], [8]]
RELAYS = [o for o in ORDER if children(GATHER, o)]


def dot_last(a, b):
    return lax.dot_general(a, b, (((1,), (1,)), ((), ())), preferred_element_type=F32)


def dot_first(a, b):
    return lax.dot_general(a, b, (((0,), (0,)), ((), ())), preferred_element_type=F32)


def dot(a, b):
    return jnp.dot(a, b, preferred_element_type=F32)


def kernel(
    pq, aq, pkv, akv, pg, ag, lens,
    packed,
    kv, qg, q_all, g_all, pp, dpp, pa, dpa, stat, ot, st, dqt, own_f, osend, orecv,
    part, sib_out, sib_in, rs_out, rs_in, fin, own_in,
    loc, kv_r, kv_s, kv_x, qg_r, qg_s, st_r, st_s, o_r, o_s, sib_r, sib_s, rs_r, rs_s, fin_r, fin_s, own_r, own_s,
):
    blk, resp = lax.axis_index("blk"), lax.axis_index("resp")
    lo, z = blk // RING, lax.rem(blk, RING)
    hi, c = resp // 2, lax.rem(resp, 2)
    x = hi * 2 + lo
    s = 1 - 2 * c
    scaling = 1.0 / math.sqrt(128)

    def ring(step):
        return {"blk": lo * RING + lax.rem(z + step + 2 * RING, RING), "resp": resp}

    def across(step, core):
        to = lax.rem(x + step + 4, 4)
        return {"blk": lax.rem(to, 2) * RING + z, "resp": (to // 2) * 2 + core}

    sibling = {"blk": blk, "resp": hi * 2 + 1 - c}

    def remote(src, dst, send, recv, to):
        return pltpu.make_async_remote_copy(
            src_ref=src, dst_ref=dst, send_sem=send, recv_sem=recv, device_id=to, device_id_type=MESH
        )

    def guard(offset, act):
        if offset == 8:
            pl.when(c == 0)(act)
        else:
            act()

    first_p = pl.multiple_of(hi * PR, PR)
    first_a = pl.multiple_of(hi * AR, AR)
    pairs = [
        (pkv.at[pl.ds(first_p, PR)], kv.at[0, pl.ds(0, PR)]),
        (akv.at[0, pl.ds(first_a, AR)], kv.at[0, pl.ds(PR, AR)]),
        (akv.at[1, pl.ds(first_a, AR)], kv.at[0, pl.ds(PR + AR, AR)]),
    ]
    for j, (p_ref, a_ref) in enumerate(((pq, aq), (pg, ag))):
        cols = pl.ds(128 * j, 128)
        pairs.append((p_ref, qg.at[x, pl.ds(0, QP), cols]))
        pairs.append((a_ref.at[0], qg.at[x, pl.ds(QP, QA), cols]))
        pairs.append((a_ref.at[1], qg.at[x, pl.ds(QP + QA, QA), cols]))
    loads = [pltpu.make_async_copy(a, b, loc.at[i]) for i, (a, b) in enumerate(pairs)]
    barrier = pltpu.get_barrier_semaphore()
    steps = sorted({o - p for o, p in GATHER.items()})
    senders = [ring(-s * d) for d in steps] + [across(d, c) for d in (1, 2, 3)] + [sibling]
    for device in senders:
        pl.semaphore_signal(barrier, inc=1, device_id=device, device_id_type=MESH)
    for load in loads:
        load.start()
    for load in loads:
        load.wait()
    pl.semaphore_wait(barrier, len(senders))

    def rows_of(piece):
        return pl.ds(*PIECES[piece])

    def hop(o, piece):
        p = GATHER[o]
        source = 0 if p == 0 else slot_of(p, c)
        mine, rows = slot_of(o, c), pl.ds(*PARCELS[piece])
        return remote(
            kv.at[source, rows], kv.at[mine, rows], kv_s.at[piece, o], kv_r.at[piece, mine], ring(s * (o - p))
        )

    def share(o, piece):
        mine, rows = slot_of(o, c), pl.ds(*PARCELS[piece])
        return remote(kv.at[mine, rows], kv.at[mine, rows], kv_x.at[piece, o], kv_r.at[piece, mine], sibling)

    def arrive(o):
        for piece in range(len(PARCELS)):
            hop(o, piece).wait_recv()
            for o2 in children(GATHER, o):
                hop(o2, piece).start()
            if o != 8:
                share(o, piece).start()

    def theirs(o):
        other = slot_of(o, 1 - c)
        for piece in range(len(PARCELS)):
            block = kv.at[other, pl.ds(*PARCELS[piece])]
            pltpu.make_async_copy(block, block, kv_r.at[piece, other]).wait()

    sends_q = [
        remote(qg.at[x], qg.at[x], qg_s.at[d], qg_r.at[d], across(d, c)) for d in (1, 2, 3)
    ]
    for d in (1, 0, 2):
        sends_q[d].start()
    for piece in range(len(PARCELS)):
        for o in children(GATHER, 0):
            hop(o, piece).start()
    for o in TAKEN[0]:
        arrive(o)
    for copy in sends_q:
        copy.wait_recv()

    for d in range(4):
        place = ((d % 2) * RING + z) * QA + lax.broadcasted_iota(jnp.int32, (QA, 128), 0)
        q_all[pl.ds(d * QP, QP)] = qg[d, pl.ds(0, QP), pl.ds(0, 128)]
        g_all[pl.ds(d * QP, QP)] = qg[d, pl.ds(0, QP), pl.ds(128, 128)]
        for k in range(2):
            rows = pl.ds(NP + k * NA + d * QA, QA)
            q_all[rows] = qg[d, pl.ds(QP + k * QA, QA), pl.ds(0, 128)]
            masked = jnp.where(
                place < lens[k + 1], qg[d, pl.ds(QP + k * QA, QA), pl.ds(128, 128)].astype(F32), 0.0
            )
            g_all[rows] = masked.astype(BF16)

    lane = lax.broadcasted_iota(jnp.int32, (1, NP), 1)
    which = (lane >= QP).astype(jnp.int32) + (lane >= 2 * QP) + (lane >= 3 * QP)
    q_place_p = (which & 1) * (RING * QP) + z * QP + lane - which * QP
    lane = lax.broadcasted_iota(jnp.int32, (1, NA), 1)
    which = (lane >= QA).astype(jnp.int32) + (lane >= 2 * QA) + (lane >= 3 * QA)
    q_place_a = (which & 1) * (RING * QA) + z * QA + lane - which * QA

    def key_ring(slot):
        off = jnp.int32(0)
        for k in range(1, 16):
            off = jnp.where(slot == k, SIGNED[k], off)
        return lo * RING + lax.rem(z + off + RING, RING)

    def kind_rows(ref, base, k):
        start, count = (0, PR) if k == 0 else (PR + (k - 1) * AR, AR)
        block = ref[pl.ds(base, WIDTH), pl.ds(start, count), :]
        return block.reshape(WIDTH * count, 256)

    iota_p = lax.broadcasted_iota(jnp.int32, (PR, NP), 0)
    iota_a = lax.broadcasted_iota(jnp.int32, (AR, NA), 0)

    def receive(g):
        for k in range(GROUPS):

            @pl.when(g == k)
            def _(k=k):
                if k:
                    for o in TAKEN[k]:
                        arrive(o)
                for o in READY[k]:
                    if o != 8:
                        theirs(o)

    def attend(g):
        base = g * WIDTH
        blocks = [key_ring(base + j) for j in range(WIDTH)]
        rows_p = kind_rows(kv, base, 0)
        keys, values = rows_p[:, :128], rows_p[:, 128:]
        sp = dot_last(keys, q_all[...]) * scaling
        causal = jnp.concatenate(
            [
                jnp.where(
                    iota_p <= q_place_p - (blocks[j] * QP + hi * PR),
                    sp[j * PR : (j + 1) * PR, :NP],
                    HIDDEN,
                )
                for j in range(WIDTH)
            ],
            axis=0,
        )
        sp = jnp.concatenate([causal, sp[:, NP:]], axis=1)
        top = jnp.max(sp, axis=0, keepdims=True)
        sa, kinds = [], []
        for k in range(2):
            rows_a = kind_rows(kv, base, k + 1)
            kinds.append(rows_a)
            sk = dot_last(rows_a[:, :128], q_all[pl.ds(NP + k * NA, NA)]) * scaling
            pieces = []
            for j in range(WIDTH):
                start = blocks[j] * QA + hi * AR
                bound = jnp.minimum(q_place_a, lens[k + 1] - 1) - start
                pieces.append(jnp.where(iota_a <= bound, sk[j * AR : (j + 1) * AR], HIDDEN))
            sa.append(jnp.concatenate(pieces, axis=0))
        tops = [top[:, :NP]]
        for k in range(2):
            a, b = NP + k * NA, NP + (k + 1) * NA
            tops.append(jnp.maximum(top[:, a:b], jnp.max(sa[k], axis=0, keepdims=True)))
        top = jnp.maximum(jnp.concatenate(tops, axis=1), FLOOR)
        wp = jnp.exp(sp - top)
        dp = dot_last(values, g_all[...])
        pp[g] = wp
        dpp[g] = dp
        total = jnp.sum(wp, axis=0, keepdims=True)
        delta = jnp.sum(wp * dp, axis=0, keepdims=True)
        out = dot_first(values, wp.astype(BF16))
        totals, deltas, outs = [total[:, :NP]], [delta[:, :NP]], [out[:, :NP]]
        for k in range(2):
            a, b = NP + k * NA, NP + (k + 1) * NA
            wa = jnp.exp(sa[k] - top[:, a:b])
            da = dot_last(kinds[k][:, 128:], g_all[pl.ds(a, NA)])
            pa[g, k] = wa
            dpa[g, k] = da
            totals.append(total[:, a:b] + jnp.sum(wa, axis=0, keepdims=True))
            deltas.append(delta[:, a:b] + jnp.sum(wa * da, axis=0, keepdims=True))
            outs.append(out[:, a:b] + dot_first(kinds[k][:, 128:], wa.astype(BF16)))
        stat[g, pl.ds(0, 1)] = top
        stat[g, pl.ds(1, 1)] = jnp.concatenate(totals, axis=1)
        stat[g, pl.ds(2, 1)] = jnp.concatenate(deltas, axis=1)
        ot[g] = jnp.concatenate(outs, axis=1)

    def forward(g, _):
        receive(g)
        attend(g)
        return 0

    lax.fori_loop(0, GROUPS, forward, 0)

    def merge(parts):
        top = functools.reduce(jnp.maximum, [p[0] for p in parts])
        factors = [jnp.exp(p[0] - top) for p in parts]
        total = sum(f * p[1] for f, p in zip(factors, parts))
        delta = sum(f * p[2] for f, p in zip(factors, parts))
        return top, total, delta, factors

    top, total, delta, factors = merge(
        [[stat[i, pl.ds(k, 1)] for k in range(3)] for i in range(GROUPS)]
    )
    st[0, 0] = top
    st[0, 1] = total
    st[0, 2] = delta
    sends_st = [
        remote(st.at[0], st.at[d], st_s.at[d], st_r.at[d], across(d, c)) for d in (1, 2, 3)
    ]
    for d in (1, 0, 2):
        sends_st[d].start()
    ot[0] = sum(f * ot[i] for i, f in enumerate(factors))
    dqt[...] = jnp.zeros_like(dqt)
    for copy in sends_st:
        copy.wait_recv()
    all_top, total, delta, _ = merge([[st[d, k] for k in range(3)] for d in range(4)])
    delta = delta / total
    scale_own = jnp.exp(top - all_top) / total
    for i in range(GROUPS):
        stat[i, pl.ds(3, 1)] = jnp.exp(stat[i, pl.ds(0, 1)] - all_top) / total

    def pass_on(o):
        mine = slot_of(o, c)
        return remote(sib_out.at[o], sib_in.at[o], sib_s.at[o], sib_r.at[o], sibling)

    def offer(o):
        def act():
            sib_out[o] = part[slot_of(o, 1 - c)].astype(BF16)
            pass_on(o).start()

        if o == 8:
            pl.when(c == 1)(act)
        else:
            act()

    def up(o, piece, direction=None):
        rows = rows_of(piece)
        step = -s * (o - REDUCE[o])
        if REDUCE[o] == 0:
            to = {"blk": lo * RING + lax.rem(z + step + 2 * RING, RING), "resp": hi * 2 + FINISHER[piece]}
        else:
            to = ring(step)
        way = c if direction is None else direction
        return remote(
            rs_out.at[o, rows], rs_in.at[way, o, rows], rs_s.at[piece, o], rs_r.at[way, piece, o], to
        )

    def send_up(o):
        def act():
            pass_on(o).wait_recv()
            mine = slot_of(o, c)
            for piece in range(len(PIECES)):
                rows = rows_of(piece)
                value = part[mine, rows] + sib_in[o, rows].astype(F32)
                for o2 in children(REDUCE, o):
                    if o2 < 8:
                        up(o2, piece).wait_recv()
                        value = value + rs_in[c, o2, rows].astype(F32)
                if 8 in children(REDUCE, o):
                    part[mine, rows] = value

                    @pl.when(c == 0)
                    def _(piece=piece, rows=rows):
                        up(8, piece).wait_recv()
                        part[mine, rows] = part[mine, rows] + rs_in[0, 8, rows].astype(F32)

                    value = part[mine, rows]
                rs_out[o, rows] = value.astype(BF16)
                up(o, piece).start()

        guard(o, act)

    def differentiate(g):
        base = g * WIDTH
        rows_p = kind_rows(kv, base, 0)
        keys = rows_p[:, :128]
        factor = stat[g, pl.ds(3, 1)]
        w = pp[g] * factor
        ds = (w * (dpp[g] - delta)).astype(BF16)
        part[pl.ds(base, WIDTH), pl.ds(0, PR), pl.ds(0, 128)] = dot(ds, q_all[...]).reshape(
            WIDTH, PR, 128
        )
        part[pl.ds(base, WIDTH), pl.ds(0, PR), pl.ds(128, 128)] = dot(
            w.astype(BF16), g_all[...]
        ).reshape(WIDTH, PR, 128)
        dq = dot_first(keys, ds)
        dqs = [dq[:, :NP]]
        for k in range(2):
            a, b = NP + k * NA, NP + (k + 1) * NA
            rows_a = kind_rows(kv, base, k + 1)
            w = pa[g, k] * factor[:, a:b]
            ds = (w * (dpa[g, k] - delta[:, a:b])).astype(BF16)
            where = pl.ds(PR + k * AR, AR)
            part[pl.ds(base, WIDTH), where, pl.ds(0, 128)] = dot(
                ds, q_all[pl.ds(a, NA)]
            ).reshape(WIDTH, AR, 128)
            part[pl.ds(base, WIDTH), where, pl.ds(128, 128)] = dot(
                w.astype(BF16), g_all[pl.ds(a, NA)]
            ).reshape(WIDTH, AR, 128)
            dqs.append(dq[:, a:b] + dot_first(rows_a[:, :128], ds))
        dqt[...] += jnp.concatenate(dqs, axis=1)

    def reduce(i):
        for k in range(GROUPS):

            @pl.when(i == k)
            def _(k=k):
                for o in DONE[k]:
                    offer(o)
                if k:
                    for o in DONE[k - 1]:
                        if not children(REDUCE, o):
                            send_up(o)

    def backward(i, _):
        differentiate(GROUPS - 1 - i)
        reduce(i)
        return 0

    lax.fori_loop(0, GROUPS, backward, 0)
    other = pl.multiple_of((1 - c) * PR, PR)
    swap = remote(part.at[0, pl.ds(other, WINDOW)], own_in, own_s, own_r, sibling)
    swap.start()
    for o in DONE[GROUPS - 1]:
        if not children(REDUCE, o):
            send_up(o)

    backs = []
    for j, whole in enumerate((ot[0] * scale_own, dqt[...])):
        rows = whole.T
        for d in range(4):
            for start, count, at in (
                (d * QP, QP, 0),
                (NP + d * QA, QA, QP),
                (NP + NA + d * QA, QA, QP + QA),
            ):
                piece = rows[start : start + count]
                own_f[j, d, pl.ds(at, count)] = piece
                osend[j, d, pl.ds(at, count)] = piece.astype(BF16)
        for d in (2, 1, 3):
            theirs_x = lax.rem(x + 4 - d, 4)
            back = remote(
                osend.at[j, theirs_x], orecv.at[j, d], o_s.at[j, d], o_r.at[j, d], across(-d, c)
            )
            back.start()
            backs.append(back)

    def early(o):
        return lax.rem(z - s * o + RING, RING) < 7

    for o in sorted(REDUCE, reverse=True):
        if children(REDUCE, o):
            pl.when(early(o))(lambda o=o: send_up(o))

    for back in backs:
        back.wait_recv()
    place = blk * QA + lax.broadcasted_iota(jnp.int32, (QA, 128), 0)
    for j in range(2):
        cols = pl.ds(128 * j, 128)
        value = own_f[j, x]
        for d in (1, 2, 3):
            value = value + orecv[j, d].astype(F32)
        if j:
            value = value * scaling
        packed[pl.ds(0, QP), cols] = value[:QP].astype(BF16)
        for k in range(2):
            rows = value[QP + k * QA : QP + (k + 1) * QA]
            if j == 0:
                rows = jnp.where(place < lens[k + 1], rows, 0.0)
            packed[pl.ds(QP + k * QA, QA), cols] = rows.astype(BF16)

    for o in sorted(REDUCE, reverse=True):
        if children(REDUCE, o):
            pl.when(jnp.logical_not(early(o)))(lambda o=o: send_up(o))

    swap.wait_recv()
    first = pl.multiple_of(c * PR, PR)
    window = pl.ds(first, WINDOW)
    value = part[0, window] + own_in[...]
    for o in children(REDUCE, 0)[::-1]:
        for way in range(2):
            for piece, core in enumerate(FINISHER):
                pl.when(c == core)(lambda: up(o, piece, way).wait_recv())
            value = value + rs_in[way, o, window].astype(F32)
    factor = jnp.where(lax.broadcasted_iota(jnp.int32, (1, 256), 1) < 128, scaling, 1.0)
    fin[0, c] = (value * factor).astype(BF16)
    finals = [
        remote(fin.at[0, c], fin.at[0, c], fin_s.at[0], fin_r.at[0, 0], sibling),
        remote(fin.at[0, c], fin.at[1, c], fin_s.at[1], fin_r.at[1, c], across(2, c)),
        remote(fin.at[0, c], fin.at[1, c], fin_s.at[2], fin_r.at[1, c], across(2, 1 - c)),
    ]
    for f in finals[::-1]:
        f.start()
    for h in range(2):
        half = hi if h == 0 else 1 - hi
        if h == 0:
            finals[0].wait_recv()
        else:
            for core in range(2):
                block = fin.at[1, core]
                pltpu.make_async_copy(block, block, fin_r.at[1, core]).wait()
        cols = pl.ds(256, 256)
        packed[pl.ds(pl.multiple_of(half * PR, PR), PR), cols] = fin[h, 0, pl.ds(0, PR)]
        for k in range(2):
            packed[pl.ds(pl.multiple_of(QP + k * QA + half * AR, AR), AR), cols] = fin[h, 1, pl.ds(k * AR, AR)]

    for copy in sends_q + sends_st + backs + finals + [swap]:
        copy.wait_send()
    for o in GATHER:
        for piece in range(len(PARCELS)):
            hop(o, piece).wait_send()
            if o != 8:
                share(o, piece).wait_send()

        def sent(o=o):
            for piece in range(len(PIECES)):
                up(o, piece).wait_send()

        guard(o, sent)
        if o == 8:
            pl.when(c == 1)(lambda: pass_on(8).wait_send())
        else:
            pass_on(o).wait_send()


def place(packed, *refs):
    for j in range(3):
        cols = pl.ds(128 * j, 128 if j < 2 else 256)
        refs[2 * j][...] = packed[pl.ds(0, QP), cols]
        for k in range(2):
            refs[2 * j + 1][k] = packed[pl.ds(QP + k * QA, QA), cols]


def body(*args):
    vmem = pl.BlockSpec(memory_space=pltpu.VMEM)
    hbm = pl.BlockSpec(memory_space=pl.ANY)
    dma = pltpu.SemaphoreType.DMA
    outs = (
        jax.ShapeDtypeStruct((QP, 128), BF16),
        jax.ShapeDtypeStruct((2, QA, 128), BF16),
        jax.ShapeDtypeStruct((QP, 128), BF16),
        jax.ShapeDtypeStruct((2, QA, 128), BF16),
        jax.ShapeDtypeStruct((QP, 256), BF16),
        jax.ShapeDtypeStruct((2, QA, 256), BF16),
    )
    results = pl.pallas_call(
        kernel,
        out_shape=jax.ShapeDtypeStruct((OWN, 512), BF16),
        in_specs=[hbm] * 6 + [pl.BlockSpec(memory_space=pltpu.SMEM)],
        out_specs=vmem,
        scratch_shapes=[
            pltpu.VMEM((16, BLOCK, 256), BF16),
            pltpu.VMEM((4, OWN, 256), BF16),
            pltpu.VMEM((ROWS, 128), BF16),
            pltpu.VMEM((ROWS, 128), BF16),
            pltpu.VMEM((GROUPS, WIDTH * PR, ROWS), F32),
            pltpu.VMEM((GROUPS, WIDTH * PR, ROWS), F32),
            pltpu.VMEM((GROUPS, 2, WIDTH * AR, NA), F32),
            pltpu.VMEM((GROUPS, 2, WIDTH * AR, NA), F32),
            pltpu.VMEM((GROUPS, 8, ROWS), F32),
            pltpu.VMEM((GROUPS, 128, ROWS), F32),
            pltpu.VMEM((4, 3, 1, ROWS), F32),
            pltpu.VMEM((128, ROWS), F32),
            pltpu.VMEM((2, 4, OWN, 128), F32),
            pltpu.VMEM((2, 4, OWN, 128), BF16),
            pltpu.VMEM((2, 4, OWN, 128), BF16),
            pltpu.VMEM((16, BLOCK, 256), F32),
            pltpu.VMEM((9, BLOCK, 256), BF16),
            pltpu.VMEM((9, BLOCK, 256), BF16),
            pltpu.VMEM((9, BLOCK, 256), BF16),
            pltpu.VMEM((2, 9, BLOCK, 256), BF16),
            pltpu.VMEM((2, 2, WINDOW, 256), BF16),
            pltpu.VMEM((WINDOW, 256), F32),
            dma((9,)),
            dma((len(PARCELS), 16)),
            dma((len(PARCELS), 9)),
            dma((len(PARCELS), 9)),
            dma((4,)),
            dma((4,)),
            dma((4,)),
            dma((4,)),
            dma((2, 4)),
            dma((2, 4)),
            dma((9,)),
            dma((9,)),
            dma((2, len(PIECES), 9)),
            dma((len(PIECES), 9)),
            dma((2, 2)),
            dma((3,)),
            dma(()),
            dma(()),
        ],
        compiler_params=pltpu.CompilerParams(
            collective_id=0, has_side_effects=True, vmem_limit_bytes=56 * 2**20
        ),
    )(*args)
    return pl.pallas_call(
        place,
        out_shape=outs,
        in_specs=[vmem],
        out_specs=(vmem,) * 6,
        compiler_params=pltpu.CompilerParams(vmem_limit_bytes=56 * 2**20),
    )(results)


def solution(mesh):
    row = P(("batch", "blk"), "resp")
    answer = P("batch", "blk", "resp")
    row_kv = P(("batch", "blk"), None)
    answer_kv = P("batch", "blk", None)
    return jax.shard_map(
        body,
        mesh=mesh,
        in_specs=(row, answer, row_kv, answer_kv, row, answer, P("batch")),
        out_specs=(row, answer, row, answer, row_kv, answer_kv),
        check_vma=False,
    )
```

```python
import functools
import math

import jax
import jax.numpy as jnp
from jax import lax
from jax.experimental import pallas as pl
from jax.experimental.pallas import tpu as pltpu
from jax.sharding import PartitionSpec as P

MESH = pl.DeviceIdType.MESH
F32 = jnp.float32
BF16 = jnp.bfloat16
HIDDEN = -1e30
FLOOR = -1e20
RING = 16
PR, AR = 48, 32
BLOCK = PR + 2 * AR
QP, QA = 96, 64
OWN = QP + 2 * QA
ROWS = 4 * OWN
NP, NA = 4 * QP, 4 * QA
PARCELS = ((0, PR), (PR, 2 * AR))
PIECES = ((0, PR), (PR, 2 * AR))
FINISHER = (0, 1)
WINDOW = 2 * AR
GROUPS, WIDTH = 4, 4

GATHER = {1: 0, 3: 0, 2: 3, 4: 3, 6: 3, 5: 6, 7: 6, 8: 6}
REDUCE = {1: 0, 3: 0, 6: 0, 2: 3, 4: 3, 5: 6, 7: 6, 8: 6}
ORDER = [1, 3, 2, 4, 6, 5, 7]


def children(tree, parent):
    return sorted([o for o, p in tree.items() if p == parent], reverse=True)


SIGNED = [0] * 16
for _i, _o in enumerate(ORDER):
    SIGNED[1 + 2 * _i], SIGNED[2 + 2 * _i] = -_o, _o
SIGNED[15] = 8


def slot_of(offset, core):
    if offset == 8:
        return 15
    return 1 + 2 * ORDER.index(offset) + core


READY = [[o for o in GATHER if min(slot_of(o, 0), 15) // WIDTH == k] for k in range(GROUPS)]
DONE = READY[::-1]
TAKEN = [[3, 1, 6, 2, 4], [], [5, 7], [8]]
RELAYS = [o for o in ORDER if children(GATHER, o)]


def dot_last(a, b):
    return lax.dot_general(a, b, (((1,), (1,)), ((), ())), preferred_element_type=F32)


def dot_first(a, b):
    return lax.dot_general(a, b, (((0,), (0,)), ((), ())), preferred_element_type=F32)


def dot(a, b):
    return jnp.dot(a, b, preferred_element_type=F32)


def kernel(
    pq, aq, pkv, akv, pg, ag, lens,
    packed,
    kv, qg, q_all, g_all, pp, dpp, pa, dpa, stat, ot, st, dqt, own_f, osend, orecv,
    part, sib_out, sib_in, rs_out, rs_in, fin, own_in,
    loc, kv_r, kv_s, kv_x, qg_r, qg_s, st_r, st_s, o_r, o_s, sib_r, sib_s, rs_r, rs_s, fin_r, fin_s, own_r, own_s,
):
    blk, resp = lax.axis_index("blk"), lax.axis_index("resp")
    lo, z = blk // RING, lax.rem(blk, RING)
    hi, c = resp // 2, lax.rem(resp, 2)
    x = hi * 2 + lo
    s = 1 - 2 * c
    scaling = 1.0 / math.sqrt(128)

    def ring(step):
        return {"blk": lo * RING + lax.rem(z + step + 2 * RING, RING), "resp": resp}

    def across(step, core):
        to = lax.rem(x + step + 4, 4)
        return {"blk": lax.rem(to, 2) * RING + z, "resp": (to // 2) * 2 + core}

    sibling = {"blk": blk, "resp": hi * 2 + 1 - c}

    def remote(src, dst, send, recv, to):
        return pltpu.make_async_remote_copy(
            src_ref=src, dst_ref=dst, send_sem=send, recv_sem=recv, device_id=to, device_id_type=MESH
        )

    def guard(offset, act):
        if offset == 8:
            pl.when(c == 0)(act)
        else:
            act()

    first_p = pl.multiple_of(hi * PR, PR)
    first_a = pl.multiple_of(hi * AR, AR)
    pairs = [
        (pkv.at[pl.ds(first_p, PR)], kv.at[0, pl.ds(0, PR)]),
        (akv.at[0, pl.ds(first_a, AR)], kv.at[0, pl.ds(PR, AR)]),
        (akv.at[1, pl.ds(first_a, AR)], kv.at[0, pl.ds(PR + AR, AR)]),
    ]
    for j, (p_ref, a_ref) in enumerate(((pq, aq), (pg, ag))):
        cols = pl.ds(128 * j, 128)
        pairs.append((p_ref, qg.at[x, pl.ds(0, QP), cols]))
        pairs.append((a_ref.at[0], qg.at[x, pl.ds(QP, QA), cols]))
        pairs.append((a_ref.at[1], qg.at[x, pl.ds(QP + QA, QA), cols]))
    loads = [pltpu.make_async_copy(a, b, loc.at[i]) for i, (a, b) in enumerate(pairs)]
    barrier = pltpu.get_barrier_semaphore()
    steps = sorted({o - p for o, p in GATHER.items()})
    senders = [ring(-s * d) for d in steps] + [across(d, c) for d in (1, 2, 3)] + [sibling]
    for device in senders:
        pl.semaphore_signal(barrier, inc=1, device_id=device, device_id_type=MESH)
    for load in loads:
        load.start()
    for load in loads:
        load.wait()
    pl.semaphore_wait(barrier, len(senders))

    def rows_of(piece):
        return pl.ds(*PIECES[piece])

    def hop(o, piece):
        p = GATHER[o]
        source = 0 if p == 0 else slot_of(p, c)
        mine, rows = slot_of(o, c), pl.ds(*PARCELS[piece])
        return remote(
            kv.at[source, rows], kv.at[mine, rows], kv_s.at[piece, o], kv_r.at[piece, mine], ring(s * (o - p))
        )

    def share(o, piece):
        mine, rows = slot_of(o, c), pl.ds(*PARCELS[piece])
        return remote(kv.at[mine, rows], kv.at[mine, rows], kv_x.at[piece, o], kv_r.at[piece, mine], sibling)

    def arrive(o):
        for piece in range(len(PARCELS)):
            hop(o, piece).wait_recv()
            for o2 in children(GATHER, o):
                hop(o2, piece).start()
            if o != 8:
                share(o, piece).start()

    def theirs(o):
        other = slot_of(o, 1 - c)
        for piece in range(len(PARCELS)):
            block = kv.at[other, pl.ds(*PARCELS[piece])]
            pltpu.make_async_copy(block, block, kv_r.at[piece, other]).wait()

    sends_q = [
        remote(qg.at[x], qg.at[x], qg_s.at[d], qg_r.at[d], across(d, c)) for d in (1, 2, 3)
    ]
    for d in (1, 0, 2):
        sends_q[d].start()
    for piece in range(len(PARCELS)):
        for o in children(GATHER, 0):
            hop(o, piece).start()
    for o in TAKEN[0]:
        arrive(o)
    for copy in sends_q:
        copy.wait_recv()

    for d in range(4):
        place = ((d % 2) * RING + z) * QA + lax.broadcasted_iota(jnp.int32, (QA, 128), 0)
        q_all[pl.ds(d * QP, QP)] = qg[d, pl.ds(0, QP), pl.ds(0, 128)]
        g_all[pl.ds(d * QP, QP)] = qg[d, pl.ds(0, QP), pl.ds(128, 128)]
        for k in range(2):
            rows = pl.ds(NP + k * NA + d * QA, QA)
            q_all[rows] = qg[d, pl.ds(QP + k * QA, QA), pl.ds(0, 128)]
            masked = jnp.where(
                place < lens[k + 1], qg[d, pl.ds(QP + k * QA, QA), pl.ds(128, 128)].astype(F32), 0.0
            )
            g_all[rows] = masked.astype(BF16)

    lane = lax.broadcasted_iota(jnp.int32, (1, NP), 1)
    which = (lane >= QP).astype(jnp.int32) + (lane >= 2 * QP) + (lane >= 3 * QP)
    q_place_p = (which & 1) * (RING * QP) + z * QP + lane - which * QP
    lane = lax.broadcasted_iota(jnp.int32, (1, NA), 1)
    which = (lane >= QA).astype(jnp.int32) + (lane >= 2 * QA) + (lane >= 3 * QA)
    q_place_a = (which & 1) * (RING * QA) + z * QA + lane - which * QA

    def key_ring(slot):
        off = jnp.int32(0)
        for k in range(1, 16):
            off = jnp.where(slot == k, SIGNED[k], off)
        return lo * RING + lax.rem(z + off + RING, RING)

    def kind_rows(ref, base, k):
        start, count = (0, PR) if k == 0 else (PR + (k - 1) * AR, AR)
        block = ref[pl.ds(base, WIDTH), pl.ds(start, count), :]
        return block.reshape(WIDTH * count, 256)

    iota_p = lax.broadcasted_iota(jnp.int32, (PR, NP), 0)
    iota_a = lax.broadcasted_iota(jnp.int32, (AR, NA), 0)

    def receive(g):
        for k in range(GROUPS):

            @pl.when(g == k)
            def _(k=k):
                if k:
                    for o in TAKEN[k]:
                        arrive(o)
                for o in READY[k]:
                    if o != 8:
                        theirs(o)

    def attend(g):
        base = g * WIDTH
        blocks = [key_ring(base + j) for j in range(WIDTH)]
        rows_p = kind_rows(kv, base, 0)
        keys, values = rows_p[:, :128], rows_p[:, 128:]
        sp = dot_last(keys, q_all[...]) * scaling
        causal = jnp.concatenate(
            [
                jnp.where(
                    iota_p <= q_place_p - (blocks[j] * QP + hi * PR),
                    sp[j * PR : (j + 1) * PR, :NP],
                    HIDDEN,
                )
                for j in range(WIDTH)
            ],
            axis=0,
        )
        sp = jnp.concatenate([causal, sp[:, NP:]], axis=1)
        top = jnp.max(sp, axis=0, keepdims=True)
        sa, kinds = [], []
        for k in range(2):
            rows_a = kind_rows(kv, base, k + 1)
            kinds.append(rows_a)
            sk = dot_last(rows_a[:, :128], q_all[pl.ds(NP + k * NA, NA)]) * scaling
            pieces = []
            for j in range(WIDTH):
                start = blocks[j] * QA + hi * AR
                bound = jnp.minimum(q_place_a, lens[k + 1] - 1) - start
                pieces.append(jnp.where(iota_a <= bound, sk[j * AR : (j + 1) * AR], HIDDEN))
            sa.append(jnp.concatenate(pieces, axis=0))
        tops = [top[:, :NP]]
        for k in range(2):
            a, b = NP + k * NA, NP + (k + 1) * NA
            tops.append(jnp.maximum(top[:, a:b], jnp.max(sa[k], axis=0, keepdims=True)))
        top = jnp.maximum(jnp.concatenate(tops, axis=1), FLOOR)
        wp = jnp.exp(sp - top)
        dp = dot_last(values, g_all[...])
        pp[g] = wp
        dpp[g] = dp
        total = jnp.sum(wp, axis=0, keepdims=True)
        delta = jnp.sum(wp * dp, axis=0, keepdims=True)
        totals, deltas = [total[:, :NP]], [delta[:, :NP]]
        for k in range(2):
            a, b = NP + k * NA, NP + (k + 1) * NA
            wa = jnp.exp(sa[k] - top[:, a:b])
            da = dot_last(kinds[k][:, 128:], g_all[pl.ds(a, NA)])
            pa[g, k] = wa
            dpa[g, k] = da
            totals.append(total[:, a:b] + jnp.sum(wa, axis=0, keepdims=True))
            deltas.append(delta[:, a:b] + jnp.sum(wa * da, axis=0, keepdims=True))
        stat[g, pl.ds(0, 1)] = top
        stat[g, pl.ds(1, 1)] = jnp.concatenate(totals, axis=1)
        stat[g, pl.ds(2, 1)] = jnp.concatenate(deltas, axis=1)

    def forward(g, _):
        receive(g)
        attend(g)
        return 0

    lax.fori_loop(0, GROUPS, forward, 0)

    def merge(parts):
        top = functools.reduce(jnp.maximum, [p[0] for p in parts])
        factors = [jnp.exp(p[0] - top) for p in parts]
        total = sum(f * p[1] for f, p in zip(factors, parts))
        delta = sum(f * p[2] for f, p in zip(factors, parts))
        return top, total, delta, factors

    top, total, delta, _ = merge(
        [[stat[i, pl.ds(k, 1)] for k in range(3)] for i in range(GROUPS)]
    )
    st[0, 0] = top
    st[0, 1] = total
    st[0, 2] = delta
    sends_st = [
        remote(st.at[0], st.at[d], st_s.at[d], st_r.at[d], across(d, c)) for d in (1, 2, 3)
    ]
    for d in (1, 0, 2):
        sends_st[d].start()
    dqt[...] = jnp.zeros_like(dqt)
    ot[...] = jnp.zeros_like(ot)
    for copy in sends_st:
        copy.wait_recv()
    all_top, total, delta, _ = merge([[st[d, k] for k in range(3)] for d in range(4)])
    delta = delta / total
    for i in range(GROUPS):
        stat[i, pl.ds(3, 1)] = jnp.exp(stat[i, pl.ds(0, 1)] - all_top) / total

    def pass_on(o):
        mine = slot_of(o, c)
        return remote(sib_out.at[o], sib_in.at[o], sib_s.at[o], sib_r.at[o], sibling)

    def offer(o):
        def act():
            sib_out[o] = part[slot_of(o, 1 - c)].astype(BF16)
            pass_on(o).start()

        if o == 8:
            pl.when(c == 1)(act)
        else:
            act()

    def up(o, piece, direction=None):
        rows = rows_of(piece)
        step = -s * (o - REDUCE[o])
        if REDUCE[o] == 0:
            to = {"blk": lo * RING + lax.rem(z + step + 2 * RING, RING), "resp": hi * 2 + FINISHER[piece]}
        else:
            to = ring(step)
        way = c if direction is None else direction
        return remote(
            rs_out.at[o, rows], rs_in.at[way, o, rows], rs_s.at[piece, o], rs_r.at[way, piece, o], to
        )

    def send_up(o):
        def act():
            pass_on(o).wait_recv()
            mine = slot_of(o, c)
            for piece in range(len(PIECES)):
                rows = rows_of(piece)
                value = part[mine, rows] + sib_in[o, rows].astype(F32)
                for o2 in children(REDUCE, o):
                    if o2 < 8:
                        up(o2, piece).wait_recv()
                        value = value + rs_in[c, o2, rows].astype(F32)
                if 8 in children(REDUCE, o):
                    part[mine, rows] = value

                    @pl.when(c == 0)
                    def _(piece=piece, rows=rows):
                        up(8, piece).wait_recv()
                        part[mine, rows] = part[mine, rows] + rs_in[0, 8, rows].astype(F32)

                    value = part[mine, rows]
                rs_out[o, rows] = value.astype(BF16)
                up(o, piece).start()

        guard(o, act)

    def differentiate(g):
        base = g * WIDTH
        rows_p = kind_rows(kv, base, 0)
        keys, values = rows_p[:, :128], rows_p[:, 128:]
        factor = stat[g, pl.ds(3, 1)]
        w = pp[g] * factor
        wb = w.astype(BF16)
        ds = (w * (dpp[g] - delta)).astype(BF16)
        part[pl.ds(base, WIDTH), pl.ds(0, PR), pl.ds(0, 128)] = dot(ds, q_all[...]).reshape(
            WIDTH, PR, 128
        )
        part[pl.ds(base, WIDTH), pl.ds(0, PR), pl.ds(128, 128)] = dot(
            wb, g_all[...]
        ).reshape(WIDTH, PR, 128)
        dq = dot_first(keys, ds)
        out = dot_first(values, wb)
        dqs, outs = [dq[:, :NP]], [out[:, :NP]]
        for k in range(2):
            a, b = NP + k * NA, NP + (k + 1) * NA
            rows_a = kind_rows(kv, base, k + 1)
            w = pa[g, k] * factor[:, a:b]
            wb = w.astype(BF16)
            ds = (w * (dpa[g, k] - delta[:, a:b])).astype(BF16)
            where = pl.ds(PR + k * AR, AR)
            part[pl.ds(base, WIDTH), where, pl.ds(0, 128)] = dot(
                ds, q_all[pl.ds(a, NA)]
            ).reshape(WIDTH, AR, 128)
            part[pl.ds(base, WIDTH), where, pl.ds(128, 128)] = dot(
                wb, g_all[pl.ds(a, NA)]
            ).reshape(WIDTH, AR, 128)
            dqs.append(dq[:, a:b] + dot_first(rows_a[:, :128], ds))
            outs.append(out[:, a:b] + dot_first(rows_a[:, 128:], wb))
        dqt[...] += jnp.concatenate(dqs, axis=1)
        ot[...] += jnp.concatenate(outs, axis=1)

    def reduce(i):
        for k in range(GROUPS):

            @pl.when(i == k)
            def _(k=k):
                for o in DONE[k]:
                    offer(o)
                if k:
                    for o in DONE[k - 1]:
                        if not children(REDUCE, o):
                            send_up(o)

    def backward(i, _):
        differentiate(GROUPS - 1 - i)
        reduce(i)
        return 0

    lax.fori_loop(0, GROUPS, backward, 0)
    other = pl.multiple_of((1 - c) * PR, PR)
    swap = remote(part.at[0, pl.ds(other, WINDOW)], own_in, own_s, own_r, sibling)
    swap.start()
    for o in DONE[GROUPS - 1]:
        if not children(REDUCE, o):
            send_up(o)

    backs = []
    for j, whole in enumerate((ot[...], dqt[...])):
        rows = whole.T
        for d in range(4):
            for start, count, at in (
                (d * QP, QP, 0),
                (NP + d * QA, QA, QP),
                (NP + NA + d * QA, QA, QP + QA),
            ):
                piece = rows[start : start + count]
                own_f[j, d, pl.ds(at, count)] = piece
                osend[j, d, pl.ds(at, count)] = piece.astype(BF16)
        for d in (2, 1, 3):
            theirs_x = lax.rem(x + 4 - d, 4)
            back = remote(
                osend.at[j, theirs_x], orecv.at[j, d], o_s.at[j, d], o_r.at[j, d], across(-d, c)
            )
            back.start()
            backs.append(back)

    def early(o):
        return lax.rem(z - s * o + RING, RING) < 7

    for o in sorted(REDUCE, reverse=True):
        if children(REDUCE, o):
            pl.when(early(o))(lambda o=o: send_up(o))

    for back in backs:
        back.wait_recv()
    place = blk * QA + lax.broadcasted_iota(jnp.int32, (QA, 128), 0)
    for j in range(2):
        cols = pl.ds(128 * j, 128)
        value = own_f[j, x]
        for d in (1, 2, 3):
            value = value + orecv[j, d].astype(F32)
        if j:
            value = value * scaling
        packed[pl.ds(0, QP), cols] = value[:QP].astype(BF16)
        for k in range(2):
            rows = value[QP + k * QA : QP + (k + 1) * QA]
            if j == 0:
                rows = jnp.where(place < lens[k + 1], rows, 0.0)
            packed[pl.ds(QP + k * QA, QA), cols] = rows.astype(BF16)

    for o in sorted(REDUCE, reverse=True):
        if children(REDUCE, o):
            pl.when(jnp.logical_not(early(o)))(lambda o=o: send_up(o))

    swap.wait_recv()
    first = pl.multiple_of(c * PR, PR)
    window = pl.ds(first, WINDOW)
    value = part[0, window] + own_in[...]
    for o in children(REDUCE, 0)[::-1]:
        for way in range(2):
            for piece, core in enumerate(FINISHER):
                pl.when(c == core)(lambda: up(o, piece, way).wait_recv())
            value = value + rs_in[way, o, window].astype(F32)
    factor = jnp.where(lax.broadcasted_iota(jnp.int32, (1, 256), 1) < 128, scaling, 1.0)
    fin[0, c] = (value * factor).astype(BF16)
    finals = [
        remote(fin.at[0, c], fin.at[0, c], fin_s.at[0], fin_r.at[0, 0], sibling),
        remote(fin.at[0, c], fin.at[1, c], fin_s.at[1], fin_r.at[1, c], across(2, c)),
        remote(fin.at[0, c], fin.at[1, c], fin_s.at[2], fin_r.at[1, c], across(2, 1 - c)),
    ]
    for f in finals[::-1]:
        f.start()
    for h in range(2):
        half = hi if h == 0 else 1 - hi
        if h == 0:
            finals[0].wait_recv()
        else:
            for core in range(2):
                block = fin.at[1, core]
                pltpu.make_async_copy(block, block, fin_r.at[1, core]).wait()
        cols = pl.ds(256, 256)
        packed[pl.ds(pl.multiple_of(half * PR, PR), PR), cols] = fin[h, 0, pl.ds(0, PR)]
        for k in range(2):
            packed[pl.ds(pl.multiple_of(QP + k * QA + half * AR, AR), AR), cols] = fin[h, 1, pl.ds(k * AR, AR)]

    for copy in sends_q + sends_st + backs + finals + [swap]:
        copy.wait_send()
    for o in GATHER:
        for piece in range(len(PARCELS)):
            hop(o, piece).wait_send()
            if o != 8:
                share(o, piece).wait_send()

        def sent(o=o):
            for piece in range(len(PIECES)):
                up(o, piece).wait_send()

        guard(o, sent)
        if o == 8:
            pl.when(c == 1)(lambda: pass_on(8).wait_send())
        else:
            pass_on(o).wait_send()


def place(packed, *refs):
    for j in range(3):
        cols = pl.ds(128 * j, 128 if j < 2 else 256)
        refs[2 * j][...] = packed[pl.ds(0, QP), cols]
        for k in range(2):
            refs[2 * j + 1][k] = packed[pl.ds(QP + k * QA, QA), cols]


def body(*args):
    vmem = pl.BlockSpec(memory_space=pltpu.VMEM)
    hbm = pl.BlockSpec(memory_space=pl.ANY)
    dma = pltpu.SemaphoreType.DMA
    outs = (
        jax.ShapeDtypeStruct((QP, 128), BF16),
        jax.ShapeDtypeStruct((2, QA, 128), BF16),
        jax.ShapeDtypeStruct((QP, 128), BF16),
        jax.ShapeDtypeStruct((2, QA, 128), BF16),
        jax.ShapeDtypeStruct((QP, 256), BF16),
        jax.ShapeDtypeStruct((2, QA, 256), BF16),
    )
    results = pl.pallas_call(
        kernel,
        out_shape=jax.ShapeDtypeStruct((OWN, 512), BF16),
        in_specs=[hbm] * 6 + [pl.BlockSpec(memory_space=pltpu.SMEM)],
        out_specs=vmem,
        scratch_shapes=[
            pltpu.VMEM((16, BLOCK, 256), BF16),
            pltpu.VMEM((4, OWN, 256), BF16),
            pltpu.VMEM((ROWS, 128), BF16),
            pltpu.VMEM((ROWS, 128), BF16),
            pltpu.VMEM((GROUPS, WIDTH * PR, ROWS), F32),
            pltpu.VMEM((GROUPS, WIDTH * PR, ROWS), F32),
            pltpu.VMEM((GROUPS, 2, WIDTH * AR, NA), F32),
            pltpu.VMEM((GROUPS, 2, WIDTH * AR, NA), F32),
            pltpu.VMEM((GROUPS, 8, ROWS), F32),
            pltpu.VMEM((128, ROWS), F32),
            pltpu.VMEM((4, 3, 1, ROWS), F32),
            pltpu.VMEM((128, ROWS), F32),
            pltpu.VMEM((2, 4, OWN, 128), F32),
            pltpu.VMEM((2, 4, OWN, 128), BF16),
            pltpu.VMEM((2, 4, OWN, 128), BF16),
            pltpu.VMEM((16, BLOCK, 256), F32),
            pltpu.VMEM((9, BLOCK, 256), BF16),
            pltpu.VMEM((9, BLOCK, 256), BF16),
            pltpu.VMEM((9, BLOCK, 256), BF16),
            pltpu.VMEM((2, 9, BLOCK, 256), BF16),
            pltpu.VMEM((2, 2, WINDOW, 256), BF16),
            pltpu.VMEM((WINDOW, 256), F32),
            dma((9,)),
            dma((len(PARCELS), 16)),
            dma((len(PARCELS), 9)),
            dma((len(PARCELS), 9)),
            dma((4,)),
            dma((4,)),
            dma((4,)),
            dma((4,)),
            dma((2, 4)),
            dma((2, 4)),
            dma((9,)),
            dma((9,)),
            dma((2, len(PIECES), 9)),
            dma((len(PIECES), 9)),
            dma((2, 2)),
            dma((3,)),
            dma(()),
            dma(()),
        ],
        compiler_params=pltpu.CompilerParams(
            collective_id=0, has_side_effects=True, vmem_limit_bytes=56 * 2**20
        ),
    )(*args)
    return pl.pallas_call(
        place,
        out_shape=outs,
        in_specs=[vmem],
        out_specs=(vmem,) * 6,
        compiler_params=pltpu.CompilerParams(vmem_limit_bytes=56 * 2**20),
    )(results)


def solution(mesh):
    row = P(("batch", "blk"), "resp")
    answer = P("batch", "blk", "resp")
    row_kv = P(("batch", "blk"), None)
    answer_kv = P("batch", "blk", None)
    return jax.shard_map(
        body,
        mesh=mesh,
        in_specs=(row, answer, row_kv, answer_kv, row, answer, P("batch")),
        out_specs=(row, answer, row, answer, row_kv, answer_kv),
        check_vma=False,
    )
```

```python
import functools
import math

import jax
import jax.numpy as jnp
from jax import lax
from jax.experimental import pallas as pl
from jax.experimental.pallas import tpu as pltpu
from jax.sharding import PartitionSpec as P

MESH = pl.DeviceIdType.MESH
F32 = jnp.float32
BF16 = jnp.bfloat16
HIDDEN = -1e30
FLOOR = -1e20
RING = 16
PR, AR = 48, 32
BLOCK = PR + 2 * AR
QP, QA = 96, 64
OWN = QP + 2 * QA
ROWS = 4 * OWN
NP, NA = 4 * QP, 4 * QA
PARCELS = ((0, PR), (PR, 2 * AR))
PIECES = ((0, PR), (PR, 2 * AR))
FINISHER = (0, 1)
WINDOW = 2 * AR
GROUPS, WIDTH = 4, 4

GATHER = {1: 0, 3: 0, 2: 3, 4: 3, 6: 3, 5: 6, 7: 6, 8: 6}
REDUCE = {1: 0, 3: 0, 6: 0, 2: 3, 4: 3, 5: 6, 7: 6, 8: 6}
ORDER = [1, 3, 2, 4, 6, 5, 7]


def children(tree, parent):
    return sorted([o for o, p in tree.items() if p == parent], reverse=True)


SIGNED = [0] * 16
for _i, _o in enumerate(ORDER):
    SIGNED[1 + 2 * _i], SIGNED[2 + 2 * _i] = -_o, _o
SIGNED[15] = 8


def slot_of(offset, core):
    if offset == 8:
        return 15
    return 1 + 2 * ORDER.index(offset) + core


READY = [[o for o in GATHER if min(slot_of(o, 0), 15) // WIDTH == k] for k in range(GROUPS)]
DONE = READY[::-1]
TAKEN = [[3, 1, 6, 2, 4], [], [5, 7], [8]]
RELAYS = [o for o in ORDER if children(GATHER, o)]


def dot_last(a, b):
    return lax.dot_general(a, b, (((1,), (1,)), ((), ())), preferred_element_type=F32)


def dot_first(a, b):
    return lax.dot_general(a, b, (((0,), (0,)), ((), ())), preferred_element_type=F32)


def dot(a, b):
    return jnp.dot(a, b, preferred_element_type=F32)


def kernel(
    pq, aq, pkv, akv, pg, ag, lens,
    packed,
    kv, qg, q_all, g_all, pp, dpp, pa, dpa, stat, ot, st, dqt, own_f, osend, orecv,
    part, sib_out, sib_in, rs_out, rs_in, fin, own_in,
    loc, kv_r, kv_s, kv_x, qg_r, qg_s, st_r, st_s, o_r, o_s, sib_r, sib_s, rs_r, rs_s, fin_r, fin_s, own_r, own_s,
):
    blk, resp = lax.axis_index("blk"), lax.axis_index("resp")
    lo, z = blk // RING, lax.rem(blk, RING)
    hi, c = resp // 2, lax.rem(resp, 2)
    x = hi * 2 + lo
    s = 1 - 2 * c
    scaling = 1.0 / math.sqrt(128)

    def ring(step):
        return {"blk": lo * RING + lax.rem(z + step + 2 * RING, RING), "resp": resp}

    def across(step, core):
        to = lax.rem(x + step + 4, 4)
        return {"blk": lax.rem(to, 2) * RING + z, "resp": (to // 2) * 2 + core}

    sibling = {"blk": blk, "resp": hi * 2 + 1 - c}

    def remote(src, dst, send, recv, to):
        return pltpu.make_async_remote_copy(
            src_ref=src, dst_ref=dst, send_sem=send, recv_sem=recv, device_id=to, device_id_type=MESH
        )

    def guard(offset, act):
        if offset == 8:
            pl.when(c == 0)(act)
        else:
            act()

    first_p = pl.multiple_of(hi * PR, PR)
    first_a = pl.multiple_of(hi * AR, AR)
    pairs = [
        (pkv.at[pl.ds(first_p, PR)], kv.at[0, pl.ds(0, PR)]),
        (akv.at[0, pl.ds(first_a, AR)], kv.at[0, pl.ds(PR, AR)]),
        (akv.at[1, pl.ds(first_a, AR)], kv.at[0, pl.ds(PR + AR, AR)]),
    ]
    for j, (p_ref, a_ref) in enumerate(((pq, aq), (pg, ag))):
        cols = pl.ds(128 * j, 128)
        pairs.append((p_ref, qg.at[x, pl.ds(0, QP), cols]))
        pairs.append((a_ref.at[0], qg.at[x, pl.ds(QP, QA), cols]))
        pairs.append((a_ref.at[1], qg.at[x, pl.ds(QP + QA, QA), cols]))
    loads = [pltpu.make_async_copy(a, b, loc.at[i]) for i, (a, b) in enumerate(pairs)]
    barrier = pltpu.get_barrier_semaphore()
    steps = sorted({o - p for o, p in GATHER.items()})
    senders = [ring(-s * d) for d in steps] + [across(d, c) for d in (1, 2, 3)] + [sibling]
    for device in senders:
        pl.semaphore_signal(barrier, inc=1, device_id=device, device_id_type=MESH)
    for load in loads:
        load.start()
    for load in loads:
        load.wait()
    pl.semaphore_wait(barrier, len(senders))

    def rows_of(piece):
        return pl.ds(*PIECES[piece])

    def hop(o, piece):
        p = GATHER[o]
        source = 0 if p == 0 else slot_of(p, c)
        mine, rows = slot_of(o, c), pl.ds(*PARCELS[piece])
        return remote(
            kv.at[source, rows], kv.at[mine, rows], kv_s.at[piece, o], kv_r.at[piece, mine], ring(s * (o - p))
        )

    def share(o, piece):
        mine, rows = slot_of(o, c), pl.ds(*PARCELS[piece])
        return remote(kv.at[mine, rows], kv.at[mine, rows], kv_x.at[piece, o], kv_r.at[piece, mine], sibling)

    def arrive(o):
        for piece in range(len(PARCELS)):
            hop(o, piece).wait_recv()
            for o2 in children(GATHER, o):
                hop(o2, piece).start()
            if o != 8:
                share(o, piece).start()

    def theirs(o):
        other = slot_of(o, 1 - c)
        for piece in range(len(PARCELS)):
            block = kv.at[other, pl.ds(*PARCELS[piece])]
            pltpu.make_async_copy(block, block, kv_r.at[piece, other]).wait()

    sends_q = [
        remote(qg.at[x], qg.at[x], qg_s.at[d], qg_r.at[d], across(d, c)) for d in (1, 2, 3)
    ]
    for d in (1, 0, 2):
        sends_q[d].start()
    for piece in range(len(PARCELS)):
        for o in children(GATHER, 0):
            hop(o, piece).start()
    for o in TAKEN[0]:
        arrive(o)
    dqt[...] = jnp.zeros_like(dqt)
    ot[...] = jnp.zeros_like(ot)
    for copy in sends_q:
        copy.wait_recv()

    for d in range(4):
        place = ((d % 2) * RING + z) * QA + lax.broadcasted_iota(jnp.int32, (QA, 128), 0)
        q_all[pl.ds(d * QP, QP)] = qg[d, pl.ds(0, QP), pl.ds(0, 128)]
        g_all[pl.ds(d * QP, QP)] = qg[d, pl.ds(0, QP), pl.ds(128, 128)]
        for k in range(2):
            rows = pl.ds(NP + k * NA + d * QA, QA)
            q_all[rows] = qg[d, pl.ds(QP + k * QA, QA), pl.ds(0, 128)]
            masked = jnp.where(
                place < lens[k + 1], qg[d, pl.ds(QP + k * QA, QA), pl.ds(128, 128)].astype(F32), 0.0
            )
            g_all[rows] = masked.astype(BF16)

    lane = lax.broadcasted_iota(jnp.int32, (1, NP), 1)
    which = (lane >= QP).astype(jnp.int32) + (lane >= 2 * QP) + (lane >= 3 * QP)
    q_place_p = (which & 1) * (RING * QP) + z * QP + lane - which * QP
    lane = lax.broadcasted_iota(jnp.int32, (1, NA), 1)
    which = (lane >= QA).astype(jnp.int32) + (lane >= 2 * QA) + (lane >= 3 * QA)
    q_place_a = (which & 1) * (RING * QA) + z * QA + lane - which * QA

    def key_ring(slot):
        off = jnp.int32(0)
        for k in range(1, 16):
            off = jnp.where(slot == k, SIGNED[k], off)
        return lo * RING + lax.rem(z + off + RING, RING)

    def kind_rows(ref, base, k):
        start, count = (0, PR) if k == 0 else (PR + (k - 1) * AR, AR)
        block = ref[pl.ds(base, WIDTH), pl.ds(start, count), :]
        return block.reshape(WIDTH * count, 256)

    iota_p = lax.broadcasted_iota(jnp.int32, (PR, NP), 0)
    iota_a = lax.broadcasted_iota(jnp.int32, (AR, NA), 0)

    def receive(g):
        for k in range(GROUPS):

            @pl.when(g == k)
            def _(k=k):
                if k:
                    for o in TAKEN[k]:
                        arrive(o)
                for o in READY[k]:
                    if o != 8:
                        theirs(o)

    def attend(g):
        base = g * WIDTH
        blocks = [key_ring(base + j) for j in range(WIDTH)]
        rows_p = kind_rows(kv, base, 0)
        keys, values = rows_p[:, :128], rows_p[:, 128:]
        sp = dot_last(keys, q_all[...]) * scaling
        causal = jnp.concatenate(
            [
                jnp.where(
                    iota_p <= q_place_p - (blocks[j] * QP + hi * PR),
                    sp[j * PR : (j + 1) * PR, :NP],
                    HIDDEN,
                )
                for j in range(WIDTH)
            ],
            axis=0,
        )
        sp = jnp.concatenate([causal, sp[:, NP:]], axis=1)
        top = jnp.max(sp, axis=0, keepdims=True)
        sa, kinds = [], []
        for k in range(2):
            rows_a = kind_rows(kv, base, k + 1)
            kinds.append(rows_a)
            sk = dot_last(rows_a[:, :128], q_all[pl.ds(NP + k * NA, NA)]) * scaling
            pieces = []
            for j in range(WIDTH):
                start = blocks[j] * QA + hi * AR
                bound = jnp.minimum(q_place_a, lens[k + 1] - 1) - start
                pieces.append(jnp.where(iota_a <= bound, sk[j * AR : (j + 1) * AR], HIDDEN))
            sa.append(jnp.concatenate(pieces, axis=0))
        tops = [top[:, :NP]]
        for k in range(2):
            a, b = NP + k * NA, NP + (k + 1) * NA
            tops.append(jnp.maximum(top[:, a:b], jnp.max(sa[k], axis=0, keepdims=True)))
        top = jnp.maximum(jnp.concatenate(tops, axis=1), FLOOR)
        wp = jnp.exp(sp - top)
        dp = dot_last(values, g_all[...])
        pp[g] = wp
        dpp[g] = dp
        total = jnp.sum(wp, axis=0, keepdims=True)
        delta = jnp.sum(wp * dp, axis=0, keepdims=True)
        totals, deltas = [total[:, :NP]], [delta[:, :NP]]
        for k in range(2):
            a, b = NP + k * NA, NP + (k + 1) * NA
            wa = jnp.exp(sa[k] - top[:, a:b])
            da = dot_last(kinds[k][:, 128:], g_all[pl.ds(a, NA)])
            pa[g, k] = wa
            dpa[g, k] = da
            totals.append(total[:, a:b] + jnp.sum(wa, axis=0, keepdims=True))
            deltas.append(delta[:, a:b] + jnp.sum(wa * da, axis=0, keepdims=True))
        stat[g, pl.ds(0, 1)] = top
        stat[g, pl.ds(1, 1)] = jnp.concatenate(totals, axis=1)
        stat[g, pl.ds(2, 1)] = jnp.concatenate(deltas, axis=1)

    def forward(g, _):
        receive(g)
        attend(g)
        return 0

    lax.fori_loop(0, GROUPS, forward, 0)

    def merge(parts):
        top = functools.reduce(jnp.maximum, [p[0] for p in parts])
        factors = [jnp.exp(p[0] - top) for p in parts]
        total = sum(f * p[1] for f, p in zip(factors, parts))
        delta = sum(f * p[2] for f, p in zip(factors, parts))
        return top, total, delta, factors

    top, total, delta, _ = merge(
        [[stat[i, pl.ds(k, 1)] for k in range(3)] for i in range(GROUPS)]
    )
    st[0, 0] = top
    st[0, 1] = total
    st[0, 2] = delta
    sends_st = [
        remote(st.at[0], st.at[d], st_s.at[d], st_r.at[d], across(d, c)) for d in (1, 2, 3)
    ]
    for d in (1, 0, 2):
        sends_st[d].start()
    for copy in sends_st:
        copy.wait_recv()
    all_top, total, delta, _ = merge([[st[d, k] for k in range(3)] for d in range(4)])
    delta = delta / total
    for i in range(GROUPS):
        stat[i, pl.ds(3, 1)] = jnp.exp(stat[i, pl.ds(0, 1)] - all_top) / total

    def pass_on(o):
        mine = slot_of(o, c)
        return remote(sib_out.at[o], sib_in.at[o], sib_s.at[o], sib_r.at[o], sibling)

    def offer(o):
        def act():
            sib_out[o] = part[slot_of(o, 1 - c)].astype(BF16)
            pass_on(o).start()

        if o == 8:
            pl.when(c == 1)(act)
        else:
            act()

    def up(o, piece, direction=None):
        rows = rows_of(piece)
        step = -s * (o - REDUCE[o])
        if REDUCE[o] == 0:
            to = {"blk": lo * RING + lax.rem(z + step + 2 * RING, RING), "resp": hi * 2 + FINISHER[piece]}
        else:
            to = ring(step)
        way = c if direction is None else direction
        return remote(
            rs_out.at[o, rows], rs_in.at[way, o, rows], rs_s.at[piece, o], rs_r.at[way, piece, o], to
        )

    def send_up(o):
        def act():
            pass_on(o).wait_recv()
            mine = slot_of(o, c)
            for piece in range(len(PIECES)):
                rows = rows_of(piece)
                value = part[mine, rows] + sib_in[o, rows].astype(F32)
                for o2 in children(REDUCE, o):
                    if o2 < 8:
                        up(o2, piece).wait_recv()
                        value = value + rs_in[c, o2, rows].astype(F32)
                if 8 in children(REDUCE, o):
                    part[mine, rows] = value

                    @pl.when(c == 0)
                    def _(piece=piece, rows=rows):
                        up(8, piece).wait_recv()
                        part[mine, rows] = part[mine, rows] + rs_in[0, 8, rows].astype(F32)

                    value = part[mine, rows]
                rs_out[o, rows] = value.astype(BF16)
                up(o, piece).start()

        guard(o, act)

    def differentiate(g):
        base = g * WIDTH
        rows_p = kind_rows(kv, base, 0)
        keys, values = rows_p[:, :128], rows_p[:, 128:]
        factor = stat[g, pl.ds(3, 1)]
        w = pp[g] * factor
        wb = w.astype(BF16)
        ds = (w * (dpp[g] - delta)).astype(BF16)
        part[pl.ds(base, WIDTH), pl.ds(0, PR), pl.ds(0, 128)] = dot(ds, q_all[...]).reshape(
            WIDTH, PR, 128
        )
        part[pl.ds(base, WIDTH), pl.ds(0, PR), pl.ds(128, 128)] = dot(
            wb, g_all[...]
        ).reshape(WIDTH, PR, 128)
        dq = dot_first(keys, ds)
        out = dot_first(values, wb)
        dqs, outs = [dq[:, :NP]], [out[:, :NP]]
        for k in range(2):
            a, b = NP + k * NA, NP + (k + 1) * NA
            rows_a = kind_rows(kv, base, k + 1)
            w = pa[g, k] * factor[:, a:b]
            wb = w.astype(BF16)
            ds = (w * (dpa[g, k] - delta[:, a:b])).astype(BF16)
            where = pl.ds(PR + k * AR, AR)
            part[pl.ds(base, WIDTH), where, pl.ds(0, 128)] = dot(
                ds, q_all[pl.ds(a, NA)]
            ).reshape(WIDTH, AR, 128)
            part[pl.ds(base, WIDTH), where, pl.ds(128, 128)] = dot(
                wb, g_all[pl.ds(a, NA)]
            ).reshape(WIDTH, AR, 128)
            dqs.append(dq[:, a:b] + dot_first(rows_a[:, :128], ds))
            outs.append(out[:, a:b] + dot_first(rows_a[:, 128:], wb))
        dqt[...] += jnp.concatenate(dqs, axis=1)
        ot[...] += jnp.concatenate(outs, axis=1)

    def reduce(i):
        for k in range(GROUPS):

            @pl.when(i == k)
            def _(k=k):
                for o in DONE[k]:
                    offer(o)
                if k:
                    for o in DONE[k - 1]:
                        if not children(REDUCE, o):
                            send_up(o)

    def backward(i, _):
        differentiate(GROUPS - 1 - i)
        reduce(i)
        return 0

    lax.fori_loop(0, GROUPS, backward, 0)
    other = pl.multiple_of((1 - c) * PR, PR)
    swap = remote(part.at[0, pl.ds(other, WINDOW)], own_in, own_s, own_r, sibling)
    swap.start()
    for o in DONE[GROUPS - 1]:
        if not children(REDUCE, o):
            send_up(o)

    backs = []
    for j, whole in enumerate((ot[...], dqt[...])):
        rows = whole.T
        for d in range(4):
            for start, count, at in (
                (d * QP, QP, 0),
                (NP + d * QA, QA, QP),
                (NP + NA + d * QA, QA, QP + QA),
            ):
                piece = rows[start : start + count]
                own_f[j, d, pl.ds(at, count)] = piece
                osend[j, d, pl.ds(at, count)] = piece.astype(BF16)
        for d in (2, 1, 3):
            theirs_x = lax.rem(x + 4 - d, 4)
            back = remote(
                osend.at[j, theirs_x], orecv.at[j, d], o_s.at[j, d], o_r.at[j, d], across(-d, c)
            )
            back.start()
            backs.append(back)

    def early(o):
        return lax.rem(z - s * o + RING, RING) < 7

    for o in sorted(REDUCE, reverse=True):
        if children(REDUCE, o):
            pl.when(early(o))(lambda o=o: send_up(o))

    for back in backs:
        back.wait_recv()
    place = blk * QA + lax.broadcasted_iota(jnp.int32, (QA, 128), 0)
    for j in range(2):
        cols = pl.ds(128 * j, 128)
        value = own_f[j, x]
        for d in (1, 2, 3):
            value = value + orecv[j, d].astype(F32)
        if j:
            value = value * scaling
        packed[pl.ds(0, QP), cols] = value[:QP].astype(BF16)
        for k in range(2):
            rows = value[QP + k * QA : QP + (k + 1) * QA]
            if j == 0:
                rows = jnp.where(place < lens[k + 1], rows, 0.0)
            packed[pl.ds(QP + k * QA, QA), cols] = rows.astype(BF16)

    for o in sorted(REDUCE, reverse=True):
        if children(REDUCE, o):
            pl.when(jnp.logical_not(early(o)))(lambda o=o: send_up(o))

    swap.wait_recv()
    first = pl.multiple_of(c * PR, PR)
    window = pl.ds(first, WINDOW)
    value = part[0, window] + own_in[...]
    for o in children(REDUCE, 0)[::-1]:
        for way in range(2):
            for piece, core in enumerate(FINISHER):
                pl.when(c == core)(lambda: up(o, piece, way).wait_recv())
            value = value + rs_in[way, o, window].astype(F32)
    factor = jnp.where(lax.broadcasted_iota(jnp.int32, (1, 256), 1) < 128, scaling, 1.0)
    fin[0, c] = (value * factor).astype(BF16)
    finals = [
        remote(fin.at[0, c], fin.at[0, c], fin_s.at[0], fin_r.at[0, 0], sibling),
        remote(fin.at[0, c], fin.at[1, c], fin_s.at[1], fin_r.at[1, c], across(2, c)),
        remote(fin.at[0, c], fin.at[1, c], fin_s.at[2], fin_r.at[1, c], across(2, 1 - c)),
    ]
    for f in finals[::-1]:
        f.start()
    for h in range(2):
        half = hi if h == 0 else 1 - hi
        if h == 0:
            finals[0].wait_recv()
        else:
            for core in range(2):
                block = fin.at[1, core]
                pltpu.make_async_copy(block, block, fin_r.at[1, core]).wait()
        cols = pl.ds(256, 256)
        packed[pl.ds(pl.multiple_of(half * PR, PR), PR), cols] = fin[h, 0, pl.ds(0, PR)]
        for k in range(2):
            packed[pl.ds(pl.multiple_of(QP + k * QA + half * AR, AR), AR), cols] = fin[h, 1, pl.ds(k * AR, AR)]

    for copy in sends_q + sends_st + backs + finals + [swap]:
        copy.wait_send()
    for o in GATHER:
        for piece in range(len(PARCELS)):
            hop(o, piece).wait_send()
            if o != 8:
                share(o, piece).wait_send()

        def sent(o=o):
            for piece in range(len(PIECES)):
                up(o, piece).wait_send()

        guard(o, sent)
        if o == 8:
            pl.when(c == 1)(lambda: pass_on(8).wait_send())
        else:
            pass_on(o).wait_send()


def place(packed, *refs):
    for j in range(3):
        cols = pl.ds(128 * j, 128 if j < 2 else 256)
        refs[2 * j][...] = packed[pl.ds(0, QP), cols]
        for k in range(2):
            refs[2 * j + 1][k] = packed[pl.ds(QP + k * QA, QA), cols]


def body(*args):
    vmem = pl.BlockSpec(memory_space=pltpu.VMEM)
    hbm = pl.BlockSpec(memory_space=pl.ANY)
    dma = pltpu.SemaphoreType.DMA
    outs = (
        jax.ShapeDtypeStruct((QP, 128), BF16),
        jax.ShapeDtypeStruct((2, QA, 128), BF16),
        jax.ShapeDtypeStruct((QP, 128), BF16),
        jax.ShapeDtypeStruct((2, QA, 128), BF16),
        jax.ShapeDtypeStruct((QP, 256), BF16),
        jax.ShapeDtypeStruct((2, QA, 256), BF16),
    )
    results = pl.pallas_call(
        kernel,
        out_shape=jax.ShapeDtypeStruct((OWN, 512), BF16),
        in_specs=[hbm] * 6 + [pl.BlockSpec(memory_space=pltpu.SMEM)],
        out_specs=vmem,
        scratch_shapes=[
            pltpu.VMEM((16, BLOCK, 256), BF16),
            pltpu.VMEM((4, OWN, 256), BF16),
            pltpu.VMEM((ROWS, 128), BF16),
            pltpu.VMEM((ROWS, 128), BF16),
            pltpu.VMEM((GROUPS, WIDTH * PR, ROWS), F32),
            pltpu.VMEM((GROUPS, WIDTH * PR, ROWS), F32),
            pltpu.VMEM((GROUPS, 2, WIDTH * AR, NA), F32),
            pltpu.VMEM((GROUPS, 2, WIDTH * AR, NA), F32),
            pltpu.VMEM((GROUPS, 8, ROWS), F32),
            pltpu.VMEM((128, ROWS), F32),
            pltpu.VMEM((4, 3, 1, ROWS), F32),
            pltpu.VMEM((128, ROWS), F32),
            pltpu.VMEM((2, 4, OWN, 128), F32),
            pltpu.VMEM((2, 4, OWN, 128), BF16),
            pltpu.VMEM((2, 4, OWN, 128), BF16),
            pltpu.VMEM((16, BLOCK, 256), F32),
            pltpu.VMEM((9, BLOCK, 256), BF16),
            pltpu.VMEM((9, BLOCK, 256), BF16),
            pltpu.VMEM((9, BLOCK, 256), BF16),
            pltpu.VMEM((2, 9, BLOCK, 256), BF16),
            pltpu.VMEM((2, 2, WINDOW, 256), BF16),
            pltpu.VMEM((WINDOW, 256), F32),
            dma((9,)),
            dma((len(PARCELS), 16)),
            dma((len(PARCELS), 9)),
            dma((len(PARCELS), 9)),
            dma((4,)),
            dma((4,)),
            dma((4,)),
            dma((4,)),
            dma((2, 4)),
            dma((2, 4)),
            dma((9,)),
            dma((9,)),
            dma((2, len(PIECES), 9)),
            dma((len(PIECES), 9)),
            dma((2, 2)),
            dma((3,)),
            dma(()),
            dma(()),
        ],
        compiler_params=pltpu.CompilerParams(
            collective_id=0, has_side_effects=True, vmem_limit_bytes=56 * 2**20
        ),
    )(*args)
    return pl.pallas_call(
        place,
        out_shape=outs,
        in_specs=[vmem],
        out_specs=(vmem,) * 6,
        compiler_params=pltpu.CompilerParams(vmem_limit_bytes=56 * 2**20),
    )(results)


def solution(mesh):
    row = P(("batch", "blk"), "resp")
    answer = P("batch", "blk", "resp")
    row_kv = P(("batch", "blk"), None)
    answer_kv = P("batch", "blk", None)
    return jax.shard_map(
        body,
        mesh=mesh,
        in_specs=(row, answer, row_kv, answer_kv, row, answer, P("batch")),
        out_specs=(row, answer, row, answer, row_kv, answer_kv),
        check_vma=False,
    )
```
